32 devices in a mesh: cams: 32 (over z, y, x, core).
Axes of the slice: x: 2, y: 2, z: 4, core: 2. Of those that a mesh axis runs over, the one named last changes fastest.
Arguments:
- right_side: float32 [128, 288], P('cams')
- schur_tiles: float32 [128, 4, 288, 288], P('cams'), as said below
- block_cols: int32 [128, 4], P('cams'), may hold values from 0 to 127, as said below
- tile_counts: int32 [128], P('cams'), may hold values from 1 to 4, as said below
- jacobi_inverse: float32 [128, 288, 288], P('cams'), as said below
Outputs:
- camera_update: float32 [128, 288], P('cams')
- final_residual: float32 [128, 288], P('cams')
The draws below stay inside these ranges and needn't reach their ends.
Inputs may be any that keep to these rules, and one draw needn't show every extreme that they name: block_cols[g, 0] = g; the other slots of row g hold distinct blocks (g + o) mod 128 with 1 <= o <= 8. `tile_counts`: slot 0 is always live; some block row has all 4 slots live. `schur_tiles`: S, built from the tiles as in the reference program, is symmetric positive definite. `jacobi_inverse`: every tile is symmetric positive definite.
All inputs are finite; a program needn't handle non-finite values.
Results may differ from the reference program's by a relative error of at most 0.00025.
Values sent between devices are 32-bit elements; how exact they have to be, the bound alone decides.
No kernel may reach another device: no remote copies, remote signals or barrier semaphores. Data moves between devices by JAX's collectives and lax.ppermute only.
A program may use at most 64 MiB of HBM per device.

```python
import jax
import jax.numpy as jnp
from jax import lax

BW = 288
NB_DEV = 4
SLOTS = 4
BAND = 2
ITERS = 2
NB = 128


def draw_right_side(key, part):
    rows = jnp.arange(NB, dtype=jnp.float32)
    ramp = 1.0 + 2.0 * rows / max(NB - 1, 1)
    first = jax.random.fold_in(jax.random.fold_in(key, 5), 0)
    base = jnp.clip(jax.random.normal(first, (NB, BW), jnp.float32), -6.0, 6.0)
    return base * ramp[:, None]


def draw_schur_tiles(key, part):
    first, second = jax.random.split(jax.random.fold_in(key, 7))
    scale = (BW * 2.0 * SLOTS) ** (-0.5)
    noise = jnp.clip(jax.random.normal(first, (NB, SLOTS, BW, BW), jnp.float32), -4.0, 4.0) * scale
    diag_vals = jax.random.uniform(second, (NB, BW), jnp.float32, 3.0, 6.0)
    eye = (lax.broadcasted_iota(jnp.int32, (BW, BW), 0) == lax.broadcasted_iota(jnp.int32, (BW, BW), 1)).astype(jnp.float32)
    centre = 0.5 * (noise[:, 0] + jnp.swapaxes(noise[:, 0], -1, -2)) + eye[None] * diag_vals[:, :, None]
    return noise.at[:, 0].set(centre)


def draw_block_cols(key, part):
    keys = jax.random.split(jax.random.fold_in(key, 3), NB)

    def one_row(row_key):
        return jnp.sort(jax.random.permutation(row_key, BAND * NB_DEV)[:SLOTS - 1]).astype(jnp.int32) + 1
    offsets = jax.vmap(one_row)(keys)
    rows = jnp.arange(NB, dtype=jnp.int32)
    ahead = (rows[:, None] + offsets) % NB
    return jnp.concatenate([rows[:, None], ahead], axis=1).astype(jnp.int32)


def draw_tile_counts(key, part):
    first, second = jax.random.split(jax.random.fold_in(key, 9))
    counts = jax.random.randint(first, (NB,), 1, SLOTS + 1)
    where_full = jax.random.randint(second, (), 0, NB)
    return counts.at[where_full].set(SLOTS).astype(jnp.int32)


def draw_jacobi_inverse(key, part):
    first, second = jax.random.split(jax.random.fold_in(key, 13))
    scale = 0.04 * BW ** (-0.5)
    noise = jnp.clip(jax.random.normal(first, (NB, BW, BW), jnp.float32), -4.0, 4.0) * scale
    diag_vals = jax.random.uniform(second, (NB, BW), jnp.float32, 0.15, 0.3)
    eye = (lax.broadcasted_iota(jnp.int32, (BW, BW), 0) == lax.broadcasted_iota(jnp.int32, (BW, BW), 1)).astype(jnp.float32)
    return 0.5 * (noise + jnp.swapaxes(noise, -1, -2)) + eye[None] * diag_vals[:, :, None]


def setup_inputs(seed: int = 0) -> dict:
    arg_keys = jax.random.split(jax.random.key(seed), 6)
    right_side = draw_right_side(jax.random.fold_in(arg_keys[5], 71), 0)
    schur_tiles = draw_schur_tiles(jax.random.fold_in(arg_keys[5], 71), 0)
    block_cols = draw_block_cols(jax.random.fold_in(arg_keys[5], 71), 0)
    tile_counts = draw_tile_counts(jax.random.fold_in(arg_keys[5], 71), 0)
    jacobi_inverse = draw_jacobi_inverse(jax.random.fold_in(arg_keys[5], 71), 0)
    return {"right_side": right_side, "schur_tiles": schur_tiles, "block_cols": block_cols, "tile_counts": tile_counts, "jacobi_inverse": jacobi_inverse}


HIGH = lax.Precision.HIGHEST


def apply_system(schur_tiles, block_cols, tile_counts, vector):
    blocks, slots = block_cols.shape
    slot_ids = lax.broadcasted_iota(jnp.int32, (blocks, slots), 1)
    live = slot_ids < tile_counts[:, None]
    picked = vector[block_cols]
    upper = jnp.einsum("bsij,bsj->bsi", schur_tiles, picked, precision=HIGH)
    result = jnp.sum(jnp.where(live[:, :, None], upper, jnp.float32(0.0)), axis=1)
    lower = jnp.einsum("bsij,bi->bsj", schur_tiles, vector, precision=HIGH)
    lower = jnp.where((live & (slot_ids > 0))[:, :, None], lower, jnp.float32(0.0))
    spread = jnp.zeros_like(vector).at[block_cols.reshape(-1)].add(lower.reshape(blocks * slots, -1))
    return result + spread


def apply_precond(jacobi_inverse, vector):
    return jnp.einsum("bij,bj->bi", jacobi_inverse, vector, precision=HIGH)


def reference(right_side, schur_tiles, block_cols, tile_counts, jacobi_inverse):
    camera_update = jnp.zeros_like(right_side)
    final_residual = right_side
    precond = apply_precond(jacobi_inverse, final_residual)
    norm_now = jnp.sum(final_residual * precond)
    direction = precond
    for iteration in range(ITERS):
        image = apply_system(schur_tiles, block_cols, tile_counts, direction)
        alpha = norm_now / jnp.sum(direction * image)
        camera_update = camera_update + alpha * direction
        final_residual = final_residual - alpha * image
        if iteration + 1 < ITERS:
            precond = apply_precond(jacobi_inverse, final_residual)
            fresh = jnp.sum(final_residual * precond)
            direction = precond + (fresh / norm_now) * direction
            norm_now = fresh
    return camera_update, final_residual
```

```python
import functools

import jax
import jax.numpy as jnp
from jax import lax
from jax.experimental import pallas as pl
from jax.experimental.pallas import tpu as pltpu
from jax.sharding import PartitionSpec as P

AXIS = "cams"
BAND = 2
F32 = jnp.float32
VMEM_LIMIT = 40 * 2**20
TINY = 1e-30


def padded(width):
    return -(-width // 128) * 128


def iota(shape, dim):
    return lax.broadcasted_iota(jnp.int32, shape, dim)


def total(value):
    return jnp.sum(jnp.sum(value, axis=1, keepdims=True), axis=0, keepdims=True)


def lay_scalars(values, lanes, first):
    lane = iota((1, lanes), 1)
    row = jnp.zeros((1, lanes), F32)
    for i, value in enumerate(values):
        row = jnp.where(lane == first + i, value, row)
    return row


def columns_to_row(columns, width):
    lanes = padded(width)
    skew = iota((8, 128), 1) - iota((8, 128), 0)
    parts = [jnp.zeros((8, 128), F32) for _ in range(lanes // 128)]
    for i, piece in enumerate(columns):
        tile, lane = divmod(8 * i, 128)
        parts[tile] = parts[tile] + jnp.where(skew == lane, piece, 0.0)
    return jnp.sum(jnp.concatenate(parts, axis=1), axis=0, keepdims=True)


def times_row(load, row, width):
    wide = jnp.broadcast_to(row[:, :width], (8, width))
    return [
        jnp.sum(load(i) * wide, axis=1, keepdims=True) for i in range(width // 8)
    ]


def transposed_products(tiles, group, columns, slots, width):
    sums = [jnp.zeros((8, width), F32) for _ in range(slots)]
    for i, piece in enumerate(columns):
        for slot in range(slots):
            sums[slot] = sums[slot] + tiles[group, slot, 8 * i : 8 * i + 8, :] * piece
    return sums


def scatter_products(tiles, place, live, group, columns, slots, width, own, spread):
    products = transposed_products(tiles, group, columns, slots, width)
    own[group, :, :width] = products[0]
    for slot in range(1, slots):
        where = place[group, slot]
        kept = jnp.where(live[group, slot] > 0, products[slot], 0.0)
        spread[where, :, :width] = spread[where, :, :width] + kept


def upper_columns(tiles, place, live, wide, group, slots, width):
    rows = []
    for slot in range(1, slots):
        row = wide[place[group, slot], :, :width]
        rows.append(jnp.where(live[group, slot] > 0, row, 0.0))
    pieces = []
    for i in range(width // 8):
        part = tiles[group, 1, 8 * i : 8 * i + 8, :] * rows[0]
        for slot in range(2, slots):
            part = part + tiles[group, slot, 8 * i : 8 * i + 8, :] * rows[slot - 1]
        pieces.append(jnp.sum(part, axis=1, keepdims=True))
    return pieces


def position():
    me = lax.axis_index(AXIS)
    chip = me // 2
    return chip, (me - 2 * chip) == 1, (chip - 2 * (chip // 2)) == 1


def begin_kernel(blocks, slots, width, count,
                 cols, counts, right, tiles_hbm, jacobi_hbm,
                 tiles, jacobi, place, live, swap, far, near,
                 own, spread, tile_sem, jacobi_sem):
    lanes = padded(width)
    loads = []
    for g in range(blocks):
        first = pltpu.make_async_copy(jacobi_hbm.at[g], jacobi.at[g], jacobi_sem.at[g])
        second = pltpu.make_async_copy(tiles_hbm.at[g], tiles.at[g], tile_sem.at[g])
        first.start()
        second.start()
        loads.append((first, second))
    base = lax.axis_index(AXIS) * blocks
    for g in range(blocks):
        for k in range(slots):
            ahead = cols[g, k] - base
            ahead = jnp.where(ahead < 0, ahead + count * blocks, ahead)
            place[g, k] = jnp.clip(ahead, 0, (BAND + 1) * blocks - 1)
            live[g, k] = (k < counts[g]).astype(jnp.int32)
    spread[...] = jnp.zeros_like(spread)
    own[...] = jnp.zeros_like(own)
    for g in range(blocks):
        loads[g][0].wait()
        columns = times_row(
            lambda i: jacobi[g, 8 * i : 8 * i + 8, :], right[g : g + 1, :], width
        )
        swap[g : g + 1, :] = columns_to_row(columns, width)
        loads[g][1].wait()
        scatter_products(tiles, place, live, g, columns, slots, width, own, spread)
    sums = jnp.sum(spread[...], axis=1)
    swap[blocks : 2 * blocks, :] = sums[blocks : 2 * blocks]
    far[...] = sums[2 * blocks :]
    near[...] = sums[:blocks] + jnp.sum(own[...], axis=1)


def pack_kernel(blocks, swap, swapped, far, odd_out, even_out):
    _, second, odd = position()
    rows, other = swap[...], swapped[...]
    forward = far[...] + jnp.where(second, 0.0, other[blocks:])
    forward = jnp.concatenate([forward, jnp.zeros_like(forward)], axis=0)
    backward = jnp.concatenate([rows[:blocks], other[:blocks]], axis=0)
    odd_out[...] = jnp.where(odd, forward, backward)
    even_out[...] = jnp.where(odd, backward, forward)


def spread_rows(wide, rows, first):
    for i in range(rows.shape[0]):
        wide[first + i, :, :] = jnp.broadcast_to(rows[i : i + 1], wide.shape[1:])


def middle_kernel(blocks, slots, width,
                  place, live, right, tiles, jacobi, swap, swapped, odd_in, even_in, near,
                  image, swap_out, far, near_out, wide, own, spread):
    lanes = padded(width)
    _, second, odd = position()
    rows, other = swap[...], swapped[...]
    ahead = jnp.where(odd, odd_in[...], even_in[...])
    behind = jnp.where(odd, even_in[...], odd_in[...])
    spread_rows(wide, rows[:blocks], 0)
    spread_rows(wide, jnp.where(second, ahead[blocks:], other[:blocks]), blocks)
    spread_rows(wide, ahead[:blocks], 2 * blocks)
    spread[...] = jnp.zeros_like(spread)
    own[...] = jnp.zeros_like(own)
    known = near[...] + behind[:blocks] + jnp.where(second, other[blocks:], 0.0)
    for g in range(blocks):
        columns = upper_columns(tiles, place, live, wide, g, slots, width)
        image[g : g + 1, :] = known[g : g + 1] + columns_to_row(columns, width)
    q = image[...]
    size = jnp.max(jnp.max(jnp.abs(q), axis=1, keepdims=True), axis=0, keepdims=True)
    size = jnp.where(size > TINY, size, 1.0)
    scaled = q * (1.0 / size)
    for g in range(blocks):
        columns = times_row(
            lambda i: jacobi[g, 8 * i : 8 * i + 8, :], scaled[g : g + 1, :], width
        )
        swap_out[g : g + 1, :] = columns_to_row(columns, width)
        scatter_products(tiles, place, live, g, columns, slots, width, own, spread)
    sums = jnp.sum(spread[...], axis=1)
    diagonal = jnp.sum(own[...], axis=1)
    w = swap_out[:blocks, :]
    far[...] = sums[2 * blocks :]
    near_out[...] = sums[:blocks] + diagonal
    z = rows[:blocks]
    r = right[...]
    values = [
        size,
        total(r * z[:, :width]),
        total(z * q),
        total(r * w[:, :width]),
        total(scaled * w),
        total(w * (diagonal + 2.0 * sums[:blocks])),
    ]
    swap_out[blocks : 2 * blocks, :] = sums[blocks : 2 * blocks]
    swap_out[0:1, :] = w[0:1] + lay_scalars(values, lanes, width)


def gather_kernel(blocks, width, swap, swapped, far, out):
    lanes = padded(width)
    _, second, _ = position()
    rows, other = swap[...], swapped[...]

    def at(block, i):
        return block[0:1, width + i : width + i + 1]

    lane = iota((1, lanes), 1)
    mine, theirs = at(rows, 0), at(other, 0)
    scale = jnp.where(second, mine, jnp.maximum(mine, theirs))
    sent = far[...] * (mine / scale) + jnp.where(
        second, 0.0, other[blocks:] * (theirs / scale)
    )
    crossing = total(rows[blocks:, :width] * other[:blocks, :width])
    values = [
        mine,
        scale,
        at(rows, 1) + at(other, 1),
        at(rows, 2) + at(other, 2),
        at(rows, 3),
        at(rows, 4),
        at(rows, 2),
        at(rows, 5),
        jnp.where(second, 0.0, 2.0 * crossing),
        theirs,
    ]
    out[...] = jnp.broadcast_to(
        jnp.concatenate([rows[:blocks], sent], axis=0)[None], out.shape
    )
    first = jnp.where(lane < width, rows[0:1], lay_scalars(values, lanes, width))
    out[:, 0:1, :] = jnp.broadcast_to(first[None], (out.shape[0], 1, lanes))


def scalars_of(gathered, width):
    rows = gathered[:, 0:1, :]
    return lambda i: rows[:, :, width + i : width + i + 1]


def chips_total(value):
    return jnp.sum(value, axis=0)


def sums_kernel(blocks, width, gathered, out):
    chips, _, lanes = gathered.shape
    chip, _, _ = position()
    after = jnp.where(chip == chips - 1, 0, chip + 1)
    at = scalars_of(gathered[...], width)
    alpha = chips_total(at(2)) / chips_total(at(3))
    size = alpha[None] * at(0)
    sent = alpha[None] * at(1)
    paired = alpha[None] * at(9)
    fresh = chips_total(size * size * at(5) - size * at(4) - alpha[None] * at(6))
    diagonal = chips_total(
        size * size * at(7) + size * paired * at(8) - 2.0 * (size * at(0)) * at(5)
    )
    inside = (iota((2 * blocks, lanes), 0) >= blocks) & (iota((2 * blocks, lanes), 1) < width)
    edges = jnp.zeros((2 * blocks, lanes), F32)
    for e in range(chips):
        n = (e + 1) % chips
        turned = pltpu.roll(gathered[n] * size[n], blocks, 0)
        edges = edges + gathered[e] * sent[e] * turned
    edges = total(jnp.where(inside, edges, 0.0))
    ahead = gathered[after, :blocks, :] * (alpha * gathered[after, 0:1, width : width + 1])
    out[...] = jnp.zeros_like(out)
    out[:blocks, :] = ahead
    out[0:1, :] = jnp.where(
        iota((1, lanes), 1) < width,
        ahead[0:1],
        lay_scalars([fresh, diagonal + 2.0 * edges], lanes, width),
    )


def end_kernel(blocks, slots, width,
               place, live, right, tiles, first_swap, image, swap, swapped, near, gathered, last, last_swapped,
               update, residual, wide, product):
    chips, _, lanes = gathered.shape
    chip, second, _ = position()
    after = jnp.where(chip == chips - 1, 0, chip + 1)
    before = jnp.where(chip == 0, chips - 1, chip - 1)
    at = scalars_of(gathered[...], width)
    norm = chips_total(at(2))
    along = chips_total(at(3))
    alpha = norm / along
    mine = alpha * swap[0:1, width : width + 1]
    theirs = alpha * swapped[0:1, width : width + 1]
    keep = iota((blocks, lanes), 1) < width
    w = jnp.where(keep, swap[:blocks, :], 0.0) * mine
    w_other = jnp.where(keep, swapped[:blocks, :], 0.0) * theirs
    ahead = last[:blocks, :]
    spread_rows(wide, w, 0)
    spread_rows(wide, jnp.where(second, last_swapped[:blocks, :], w_other), blocks)
    spread_rows(wide, ahead, 2 * blocks)
    known = near[...] * mine
    known = known + gathered[before, blocks:, :] * (
        alpha * gathered[before, 0:1, width + 1 : width + 2]
    )
    known = known + jnp.where(second, swapped[blocks:, :] * theirs, 0.0)
    for g in range(blocks):
        columns = upper_columns(tiles, place, live, wide, g, slots, width)
        product[g : g + 1, :] = known[g : g + 1] + columns_to_row(columns, width)

    def shared(i):
        return last[0:1, width + i : width + i + 1] + last_swapped[0:1, width + i : width + i + 1]

    fresh = norm + shared(0)
    curved = along + shared(1)
    ratio = fresh / norm
    step = fresh / (curved - ratio * (fresh / alpha))
    z = first_swap[:blocks, :]
    q = image[...]
    z_next = z - w
    update[...] = (alpha * z + step * (z_next + ratio * z))[:, :width]
    r_next = right[...] - (alpha * q)[:, :width]
    residual[...] = r_next - (step * ((q - product[...]) + ratio * q))[:, :width]


def on_device(right_side, schur_tiles, block_cols, tile_counts, jacobi_inverse):
    count = lax.axis_size(AXIS)
    blocks, slots, width, _ = schur_tiles.shape
    lanes = padded(width)
    chips = count // 2
    vmem = pl.BlockSpec(memory_space=pltpu.VMEM)
    smem = pl.BlockSpec(memory_space=pltpu.SMEM)
    hbm = pl.BlockSpec(memory_space=pltpu.HBM)
    params = pltpu.CompilerParams(vmem_limit_bytes=VMEM_LIMIT)
    rows = pltpu.VMEM((2 * blocks, lanes), F32)
    half = pltpu.VMEM((blocks, lanes), F32)
    reach = (BAND + 1) * blocks
    spread = pltpu.VMEM((reach, 8, lanes), F32)
    own = pltpu.VMEM((blocks, 8, lanes), F32)
    index = pltpu.SMEM((blocks, slots), jnp.int32)

    def swap_cores(value):
        return lax.ppermute(value, AXIS, [(i, i ^ 1) for i in range(count)])

    def swap_chips(odd, value):
        pairs = []
        for i in range(count):
            chip, core = divmod(i, 2)
            step = 1 if (chip % 2 == 1) == odd else -1
            pairs.append((i, 2 * ((chip + step) % chips) + core))
        return lax.ppermute(value, AXIS, pairs)

    tiles, jacobi, place, live, swap, far, near = pl.pallas_call(
        functools.partial(begin_kernel, blocks, slots, width, count),
        in_specs=[smem, smem, vmem, hbm, hbm],
        out_specs=[vmem, vmem, smem, smem, vmem, vmem, vmem],
        out_shape=[
            pltpu.VMEM(schur_tiles.shape, F32),
            pltpu.VMEM(jacobi_inverse.shape, F32),
            index, index, rows, half, half,
        ],
        scratch_shapes=[
            own, spread,
            pltpu.SemaphoreType.DMA((blocks,)),
            pltpu.SemaphoreType.DMA((blocks,)),
        ],
        compiler_params=params,
    )(block_cols, tile_counts, right_side, schur_tiles, jacobi_inverse)
    swapped = swap_cores(swap)
    odd_out, even_out = pl.pallas_call(
        functools.partial(pack_kernel, blocks),
        in_specs=[vmem] * 3, out_specs=[vmem] * 2, out_shape=[rows, rows],
        compiler_params=params,
    )(swap, swapped, far)
    odd_in = swap_chips(True, odd_out)
    even_in = swap_chips(False, even_out)
    image, swap2, far2, near2 = pl.pallas_call(
        functools.partial(middle_kernel, blocks, slots, width),
        in_specs=[smem, smem] + [vmem] * 8, out_specs=[vmem] * 4,
        out_shape=[half, rows, half, half],
        scratch_shapes=[spread, own, spread],
        compiler_params=params,
    )(place, live, right_side, tiles, jacobi, swap, swapped, odd_in, even_in, near)
    swapped2 = swap_cores(swap2)
    sent = pl.pallas_call(
        functools.partial(gather_kernel, blocks, width),
        in_specs=[vmem] * 3, out_specs=vmem,
        out_shape=pltpu.VMEM((chips, 2 * blocks, lanes), F32),
        compiler_params=params,
    )(swap2, swapped2, far2)
    groups = [[2 * c + core for c in range(chips)] for core in range(2)]
    gathered = lax.all_to_all(sent, AXIS, 0, 0, axis_index_groups=groups)
    last = pl.pallas_call(
        functools.partial(sums_kernel, blocks, width),
        in_specs=[vmem], out_specs=vmem, out_shape=rows,
        compiler_params=params,
    )(gathered)
    last_swapped = swap_cores(last)
    return pl.pallas_call(
        functools.partial(end_kernel, blocks, slots, width),
        in_specs=[smem, smem] + [vmem] * 10, out_specs=[vmem] * 2,
        out_shape=[jax.ShapeDtypeStruct(right_side.shape, F32)] * 2,
        scratch_shapes=[spread, half],
        compiler_params=params,
    )(place, live, right_side, tiles, swap, image, swap2, swapped2, near2, gathered, last, last_swapped)


def solution(mesh):
    placed = (
        P(AXIS, None),
        P(AXIS, None, None, None),
        P(AXIS, None),
        P(AXIS),
        P(AXIS, None, None),
    )
    return jax.shard_map(
        on_device,
        mesh=mesh,
        in_specs=placed,
        out_specs=(P(AXIS, None), P(AXIS, None)),
        check_vma=False,
    )
```

```python
import functools

import jax
import jax.numpy as jnp
from jax import lax
from jax.experimental import pallas as pl
from jax.experimental.pallas import tpu as pltpu
from jax.sharding import PartitionSpec as P

AXIS = "cams"
BAND = 2
F32 = jnp.float32
VMEM_LIMIT = 40 * 2**20
TINY = 1e-30


def padded(width):
    return -(-width // 128) * 128


def iota(shape, dim):
    return lax.broadcasted_iota(jnp.int32, shape, dim)


def total(value):
    return jnp.sum(jnp.sum(value, axis=1, keepdims=True), axis=0, keepdims=True)


def lay_scalars(values, lanes, first):
    lane = iota((1, lanes), 1)
    row = jnp.zeros((1, lanes), F32)
    for i, value in enumerate(values):
        row = jnp.where(lane == first + i, value, row)
    return row


def columns_to_row(columns, width):
    lanes = padded(width)
    skew = iota((8, 128), 1) - iota((8, 128), 0)
    parts = [jnp.zeros((8, 128), F32) for _ in range(lanes // 128)]
    for i, piece in enumerate(columns):
        tile, lane = divmod(8 * i, 128)
        parts[tile] = parts[tile] + jnp.where(skew == lane, piece, 0.0)
    return jnp.sum(jnp.concatenate(parts, axis=1), axis=0, keepdims=True)


def times_row(load, row, width):
    wide = jnp.broadcast_to(row[:, :width], (8, width))
    return [
        jnp.sum(load(i) * wide, axis=1, keepdims=True) for i in range(width // 8)
    ]


def scatter_products(tiles, place, live, group, columns, slots, width, spread):
    sums = [jnp.zeros((8, width), F32) for _ in range(1, slots)]
    for i, piece in enumerate(columns):
        for slot in range(1, slots):
            part = tiles[group, slot - 1, 8 * i : 8 * i + 8, :] * piece
            sums[slot - 1] = sums[slot - 1] + part
    for slot in range(1, slots):
        where = place[group, slot]
        kept = jnp.where(live[group, slot] > 0, sums[slot - 1], 0.0)
        spread[where, :, :width] = spread[where, :, :width] + kept


def upper_columns(tiles, place, live, wide, group, slots, width):
    rows = []
    for slot in range(1, slots):
        row = wide[place[group, slot], :, :width]
        rows.append(jnp.where(live[group, slot] > 0, row, 0.0))
    pieces = []
    for i in range(width // 8):
        part = tiles[group, 0, 8 * i : 8 * i + 8, :] * rows[0]
        for slot in range(2, slots):
            part = part + tiles[group, slot - 1, 8 * i : 8 * i + 8, :] * rows[slot - 1]
        pieces.append(jnp.sum(part, axis=1, keepdims=True))
    return pieces


def where_am_i(spot):
    return spot[0], spot[1] == 1, spot[2] == 1


def begin_kernel(blocks, slots, width, count,
                 cols_hbm, counts_hbm, right_hbm, jacobi_hbm, tiles_hbm,
                 jacobi, tiles, right, place, live, spot, z, near, odd_out, even_out,
                 cols, counts, spread, sems, jacobi_sem, tile_sem):
    small = [
        pltpu.make_async_copy(counts_hbm, counts, sems.at[0]),
        pltpu.make_async_copy(cols_hbm, cols, sems.at[1]),
        pltpu.make_async_copy(right_hbm, right, sems.at[2]),
    ]

    def jacobi_copy(g):
        return pltpu.make_async_copy(jacobi_hbm.at[g], jacobi.at[g], jacobi_sem.at[g])

    def tile_copy(g, k):
        return pltpu.make_async_copy(
            tiles_hbm.at[g, k], tiles.at[g, k - 1], tile_sem.at[g, k - 1]
        )

    for copy in small:
        copy.start()
    for g in range(blocks):
        jacobi_copy(g).start()
    small[0].wait()

    @pl.loop(0, blocks)
    def _(g):
        @pl.loop(1, counts[g])
        def _(k):
            tile_copy(g, k).start()

    @pl.loop(0, blocks)
    def _(g):
        @pl.loop(counts[g], slots)
        def _(k):
            tiles[g, k - 1] = jnp.zeros((width, width), F32)

    small[1].wait()
    base = cols[0, 0]
    me = base // blocks
    spot[0] = me // 2
    spot[1] = me % 2
    spot[2] = (me // 2) % 2
    for g in range(blocks):
        for k in range(slots):
            ahead = cols[g, k] - base
            ahead = jnp.where(ahead < 0, ahead + count * blocks, ahead)
            place[g, k] = jnp.clip(ahead, 0, (BAND + 1) * blocks - 1)
            live[g, k] = (k < counts[g]).astype(jnp.int32)
    spread[...] = jnp.zeros_like(spread)
    small[2].wait()

    for g in range(blocks):
        jacobi_copy(g).wait()
        columns = times_row(
            lambda i: jacobi[g, 8 * i : 8 * i + 8, :], right[g : g + 1, :], width
        )
        z[g : g + 1, :] = columns_to_row(columns, width)

        @pl.loop(1, counts[g])
        def _(k):
            tile_copy(g, k).wait()

        scatter_products(tiles, place, live, g, columns, slots, width, spread)
    sums = jnp.sum(spread[...], axis=1)
    near[...] = sums[:blocks]
    one, two = sums[blocks : 2 * blocks], sums[2 * blocks :]
    _, _, odd = where_am_i(spot)
    rows = z[...]
    backward = jnp.concatenate([rows, rows], axis=0)
    forward = jnp.concatenate([two, one], axis=0)
    odd_out[...] = jnp.where(odd, forward, backward)
    even_out[...] = jnp.where(odd, backward, forward)


def diagonal_product(blocks, width, diagonal, rows, out):
    for g in range(blocks):
        columns = times_row(
            lambda i: diagonal[g, 8 * i : 8 * i + 8, :], rows[g : g + 1, :], width
        )
        out[g : g + 1, :] = columns_to_row(columns, width)


def first_diagonal_kernel(blocks, width, tiles_hbm, z, near, diagonal, near_out, sem):
    copies = [
        pltpu.make_async_copy(tiles_hbm.at[g, 0], diagonal.at[g], sem.at[g])
        for g in range(blocks)
    ]
    for copy in copies:
        copy.start()
    for copy in copies:
        copy.wait()
    diagonal_product(blocks, width, diagonal, z, near_out)
    near_out[...] = near_out[...] + near[...]


def relay_kernel(blocks, spot, z, near, odd_out, even_out, odd_in, even_in, out, known):
    _, second, odd = where_am_i(spot)
    forward = jnp.where(odd, odd_out[...], even_out[...])
    ahead = jnp.where(odd, odd_in[...], even_in[...])
    behind = jnp.where(odd, even_in[...], odd_in[...])
    out[:blocks, :] = jnp.where(second, z[...], ahead[:blocks])
    out[blocks:, :] = jnp.where(second, behind[blocks:], forward[blocks:])
    known[...] = near[...] + behind[:blocks]


def spread_rows(wide, rows, first):
    for i in range(rows.shape[0]):
        wide[first + i, :, :] = jnp.broadcast_to(rows[i : i + 1], wide.shape[1:])


def middle_kernel(blocks, slots, width,
                  place, live, spot, tiles, jacobi, z, known_in, odd_in, even_in, relayed, right,
                  image, swap, far, near, wide, spread):
    lanes = padded(width)
    _, _, odd = where_am_i(spot)
    ahead = jnp.where(odd, odd_in[...], even_in[...])
    spread_rows(wide, z[...], 0)
    spread_rows(wide, relayed[:blocks, :], blocks)
    spread_rows(wide, ahead[:blocks], 2 * blocks)
    spread[...] = jnp.zeros_like(spread)
    known = known_in[...] + relayed[blocks:, :]
    for g in range(blocks):
        columns = upper_columns(tiles, place, live, wide, g, slots, width)
        image[g : g + 1, :] = known[g : g + 1, :] + columns_to_row(columns, width)
    q = image[...]
    size = jnp.max(jnp.max(jnp.abs(q), axis=1, keepdims=True), axis=0, keepdims=True)
    size = jnp.where(size > TINY, size, 1.0)
    scaled = q * (1.0 / size)
    for g in range(blocks):
        columns = times_row(
            lambda i: jacobi[g, 8 * i : 8 * i + 8, :], scaled[g : g + 1, :], width
        )
        swap[g : g + 1, :] = columns_to_row(columns, width)
        scatter_products(tiles, place, live, g, columns, slots, width, spread)
    sums = jnp.sum(spread[...], axis=1)
    far[...] = sums[2 * blocks :]
    near[...] = sums[:blocks]
    swap[blocks : 2 * blocks, :] = sums[blocks : 2 * blocks]
    values = [size, total(right[...] * z[:, :width]), total(z[...] * q)]
    swap[0:1, :] = swap[0:1, :] + lay_scalars(values, lanes, width)


def second_diagonal_kernel(blocks, width, right, diagonal_tiles, image, swap, near, near_out, out):
    lanes = padded(width)
    keep = iota((blocks, lanes), 1) < width
    w = jnp.where(keep, swap[:blocks, :], 0.0)
    diagonal_product(blocks, width, diagonal_tiles, swap, near_out)
    diagonal = near_out[...]
    values = [
        total(right[...] * w[:, :width]),
        total(image[...] * w),
        total(w * (diagonal + 2.0 * near[...])),
    ]
    near_out[...] = diagonal + near[...]
    out[...] = lay_scalars(values, 128, 0)


def fold(head, other, width, extra):
    tail = width - 256
    lane = iota((head.shape[0], 128), 1)
    last = jnp.where(lane < tail, head[:, 256:384], pltpu.roll(other[:, 256:384], tail, 1))
    last = jnp.where(lane < 2 * tail, last, extra)
    return head[:, :128], head[:, 128:256], other[:, :128], other[:, 128:256], last


def unfold_first(part, width):
    tail = width - 256
    last = jnp.where(iota(part.shape[1:], 1) < tail, part[4], 0.0)
    return jnp.concatenate([part[0], part[1], last], axis=1)


def unfold_second(part, width):
    tail = width - 256
    last = jnp.where(iota(part.shape[1:], 1) < tail, pltpu.roll(part[4], 128 - tail, 1), 0.0)
    return jnp.concatenate([part[2], part[3], last], axis=1)


def gather_kernel(blocks, width, spot, swap, swapped, far, dots, out):
    _, second, _ = where_am_i(spot)
    rows, other = swap[...], swapped[...]

    def at(block, i):
        return block[0:1, width + i : width + i + 1]

    mine, theirs = at(rows, 0), at(other, 0)
    scale = jnp.where(second, mine, jnp.maximum(mine, theirs))
    sent = far[...] * (mine / scale) + jnp.where(
        second, 0.0, other[blocks:] * (theirs / scale)
    )
    crossing = total(rows[blocks:, :width] * other[:blocks, :width])
    values = [
        mine,
        scale,
        at(rows, 1) + at(other, 1),
        at(rows, 2) + at(other, 2),
        dots[0:1, 0:1],
        dots[0:1, 1:2] / mine,
        at(rows, 2),
        dots[0:1, 2:3],
        jnp.where(second, 0.0, 2.0 * crossing),
        theirs,
    ]
    extra = lay_scalars(values, 128, 2 * (width - 256))
    parts = fold(rows[:blocks], sent, width, extra)
    for e in range(out.shape[0]):
        for i, part in enumerate(parts):
            out[e, i] = part


def after_kernel(spot, gathered, out):
    chips = gathered.shape[0]
    chip, _, _ = where_am_i(spot)
    out[...] = gathered[jnp.where(chip == chips - 1, 0, chip + 1)]


def sums_kernel(blocks, width, gathered, out):
    chips = gathered.shape[0]
    tail = width - 256
    table = jnp.concatenate([gathered[e, 4, 0:1, :] for e in range(chips)], axis=0)
    later = jnp.concatenate([table[1:], table[:1]], axis=0)

    def at(i, rows=table):
        return rows[:, 2 * tail + i : 2 * tail + i + 1]

    def chips_total(value):
        return jnp.sum(value, axis=0, keepdims=True)

    norm = chips_total(at(2))
    along = chips_total(at(3))
    alpha = norm / along
    size = alpha * at(0)
    fresh = chips_total(size * (size * at(5) - at(4)) - alpha * at(6))
    diagonal = chips_total(
        size * (size * at(7) + (alpha * at(9)) * at(8) - 2.0 * at(0) * at(5))
    )
    weight = (alpha * at(1)) * (alpha * at(0, later))
    inside = iota((blocks, 128), 1) < tail
    lines = []
    for e in range(chips):
        n = (e + 1) % chips
        ends = jnp.where(inside, pltpu.roll(gathered[e, 4], 128 - tail, 1) * gathered[n, 4], 0.0)
        pair = gathered[e, 2] * gathered[n, 0] + gathered[e, 3] * gathered[n, 1] + ends
        lines.append(jnp.sum(pair, axis=0, keepdims=True))
    edges = total(jnp.concatenate(lines, axis=0) * weight)
    values = [fresh, diagonal + 2.0 * edges, norm, along]
    out[...] = jnp.broadcast_to(lay_scalars(values, 128, 0), out.shape)


def later_kernel(blocks, slots, width,
                 place, live, spot, tiles, swap, swapped, near, gathered, next_part, next_other, sums,
                 product, scaled, wide):
    chips = gathered.shape[0]
    lanes = padded(width)
    chip, second, _ = where_am_i(spot)
    tail = width - 256
    before = gathered[jnp.where(chip == 0, chips - 1, chip - 1)]
    alpha = sums[0:1, 2:3] / sums[0:1, 3:4]

    def at(part, i):
        return alpha * part[4, 0:1, 2 * tail + i : 2 * tail + i + 1]

    mine = alpha * swap[0:1, width : width + 1]
    theirs = alpha * swapped[0:1, width : width + 1]
    keep = iota((blocks, lanes), 1) < width
    w = jnp.where(keep, swap[:blocks, :], 0.0) * mine
    w_other = jnp.where(keep, swapped[:blocks, :], 0.0) * theirs
    ahead, ahead_other = next_part[...], next_other[...]
    ahead = unfold_first(ahead, width) * at(ahead, 0)
    ahead_other = unfold_first(ahead_other, width) * at(ahead_other, 0)
    scaled[...] = w
    spread_rows(wide, w, 0)
    spread_rows(wide, jnp.where(second, ahead_other, w_other), blocks)
    spread_rows(wide, ahead, 2 * blocks)
    known = near[...] * mine + unfold_second(before, width) * at(before, 1)
    product[...] = known + jnp.where(second, swapped[blocks:, :] * theirs, 0.0)

    for g in range(blocks):
        columns = upper_columns(tiles, place, live, wide, g, slots, width)
        product[g : g + 1, :] = product[g : g + 1, :] + columns_to_row(columns, width)


def end_kernel(blocks, width, right, z_ref, image, product, scaled, sums, sums_other,
               update, residual):
    def shared(i):
        return sums[0:1, i : i + 1] + sums_other[0:1, i : i + 1]

    norm, along = sums[0:1, 2:3], sums[0:1, 3:4]
    alpha = norm / along
    fresh = norm + shared(0)
    curved = along + shared(1)
    ratio = fresh / norm
    step = fresh / (curved - ratio * (fresh / alpha))
    z, q = z_ref[...], image[...]
    z_next = z - scaled[...]
    update[...] = (alpha * z + step * (z_next + ratio * z))[:, :width]
    r_next = right[...] - (alpha * q)[:, :width]
    residual[...] = r_next - (step * ((q - product[...]) + ratio * q))[:, :width]


def on_device(right_side, schur_tiles, block_cols, tile_counts, jacobi_inverse):
    count = lax.axis_size(AXIS)
    blocks, slots, width, _ = schur_tiles.shape
    lanes = padded(width)
    chips = count // 2
    vmem = pl.BlockSpec(memory_space=pltpu.VMEM)
    smem = pl.BlockSpec(memory_space=pltpu.SMEM)
    hbm = pl.BlockSpec(memory_space=pltpu.HBM)
    rows = pltpu.VMEM((2 * blocks, lanes), F32)
    half = pltpu.VMEM((blocks, lanes), F32)
    small = pltpu.VMEM((8, 128), F32)
    spread = pltpu.VMEM(((BAND + 1) * blocks, 8, lanes), F32)
    index = pltpu.SMEM((blocks, slots), jnp.int32)

    def call(kernel, sizes, in_specs, out_shape, scratch=(), work=0):
        single = not isinstance(out_shape, list)
        shapes = [out_shape] if single else out_shape
        specs = [
            smem if getattr(shape, "memory_space", None) == pltpu.SMEM else vmem
            for shape in shapes
        ]
        return pl.pallas_call(
            functools.partial(kernel, *sizes),
            in_specs=in_specs,
            out_specs=specs[0] if single else specs,
            out_shape=out_shape,
            scratch_shapes=list(scratch),
            compiler_params=pltpu.CompilerParams(vmem_limit_bytes=VMEM_LIMIT),
            cost_estimate=pl.CostEstimate(
                flops=2 * work * width * width, bytes_accessed=4 * work * width * width, transcendentals=0
            ),
        )

    def swap_cores(value):
        return lax.ppermute(value, AXIS, [(i, i ^ 1) for i in range(count)])

    def swap_chips(odd, value):
        pairs = []
        for i in range(count):
            chip, core = divmod(i, 2)
            step = 1 if (chip % 2 == 1) == odd else -1
            pairs.append((i, 2 * ((chip + step) % chips) + core))
        return lax.ppermute(value, AXIS, pairs)

    sizes = (blocks, slots, width)
    off_chip = [
        pltpu.with_memory_space_constraint(value, pltpu.HBM)
        for value in (block_cols, tile_counts, right_side, jacobi_inverse, schur_tiles)
    ]
    jacobi, tiles, right, place, live, spot, z, near, odd_out, even_out = call(
        begin_kernel, sizes + (count,), [hbm] * 5,
        [
            pltpu.VMEM(jacobi_inverse.shape, F32),
            pltpu.VMEM((blocks, slots - 1, width, width), F32),
            pltpu.VMEM(right_side.shape, F32),
            index, index, pltpu.SMEM((4,), jnp.int32),
            half, half, rows, rows,
        ],
        [
            pltpu.SMEM(block_cols.shape, jnp.int32),
            pltpu.SMEM(tile_counts.shape, jnp.int32),
            spread,
            pltpu.SemaphoreType.DMA((3,)),
            pltpu.SemaphoreType.DMA((blocks,)),
            pltpu.SemaphoreType.DMA((blocks, slots - 1)),
        ],
        work=blocks * slots,
    )(*off_chip)
    odd_in = swap_chips(True, odd_out)
    even_in = swap_chips(False, even_out)
    diagonal, near1 = call(
        first_diagonal_kernel, (blocks, width), [hbm, vmem, vmem],
        [pltpu.VMEM((blocks, width, width), F32), half],
        [pltpu.SemaphoreType.DMA((blocks,))],
        work=blocks,
    )(off_chip[4], z, near)
    relay, known = call(relay_kernel, (blocks,), [smem] + [vmem] * 6, [rows, half])(
        spot, z, near1, odd_out, even_out, odd_in, even_in
    )
    relayed = swap_cores(relay)
    image, swap, far, near2 = call(
        middle_kernel, sizes, [smem] * 3 + [vmem] * 8, [half, rows, half, half], [spread, spread],
        work=3 * blocks * slots,
    )(place, live, spot, tiles, jacobi, z, known, odd_in, even_in, relayed, right)
    swapped = swap_cores(swap)
    near3, dots = call(
        second_diagonal_kernel, (blocks, width), [vmem] * 5, [half, pltpu.VMEM((1, 128), F32)], work=blocks
    )(right, diagonal, image, swap, near2)
    sent = call(
        gather_kernel, (blocks, width), [smem] + [vmem] * 4, pltpu.VMEM((chips, 5, blocks, 128), F32)
    )(spot, swap, swapped, far, dots)
    groups = [[2 * c + core for c in range(chips)] for core in range(2)]
    gathered = lax.all_to_all(sent, AXIS, 0, 0, axis_index_groups=groups)
    next_part = call(after_kernel, (), [smem, vmem], pltpu.VMEM((5, blocks, 128), F32))(spot, gathered)
    next_other = swap_cores(next_part)
    sums = call(sums_kernel, (blocks, width), [vmem], small, work=chips)(gathered)
    sums_other = swap_cores(sums)
    product, scaled = call(
        later_kernel, sizes, [smem] * 3 + [vmem] * 8, [half, half], [spread], work=blocks * slots,
    )(place, live, spot, tiles, swap, swapped, near3, gathered, next_part, next_other, sums)
    out = jax.ShapeDtypeStruct(right_side.shape, F32)
    return call(end_kernel, (blocks, width), [vmem] * 7, [out, out])(
        right, z, image, product, scaled, sums, sums_other
    )


def solution(mesh):
    placed = (
        P(AXIS, None),
        P(AXIS, None, None, None),
        P(AXIS, None),
        P(AXIS),
        P(AXIS, None, None),
    )
    return jax.shard_map(
        on_device,
        mesh=mesh,
        in_specs=placed,
        out_specs=(P(AXIS, None), P(AXIS, None)),
        check_vma=False,
    )
```

```python
import functools

import jax
import jax.numpy as jnp
from jax import lax
from jax.experimental import pallas as pl
from jax.experimental.pallas import tpu as pltpu
from jax.sharding import PartitionSpec as P

AXIS = "cams"
BAND = 2
F32 = jnp.float32
VMEM_LIMIT = 40 * 2**20
TINY = 1e-30


def padded(width):
    return -(-width // 128) * 128


def iota(shape, dim):
    return lax.broadcasted_iota(jnp.int32, shape, dim)


def total(value):
    return jnp.sum(jnp.sum(value, axis=1, keepdims=True), axis=0, keepdims=True)


def lay_scalars(values, lanes, first):
    lane = iota((1, lanes), 1)
    row = jnp.zeros((1, lanes), F32)
    for i, value in enumerate(values):
        row = jnp.where(lane == first + i, value, row)
    return row


def columns_to_row(columns, width):
    lanes = padded(width)
    skew = iota((8, 128), 1) - iota((8, 128), 0)
    parts = [jnp.zeros((8, 128), F32) for _ in range(lanes // 128)]
    for i, piece in enumerate(columns):
        tile, lane = divmod(8 * i, 128)
        parts[tile] = parts[tile] + jnp.where(skew == lane, piece, 0.0)
    return jnp.sum(jnp.concatenate(parts, axis=1), axis=0, keepdims=True)


def times_row(load, row, width):
    wide = jnp.broadcast_to(row[:, :width], (8, width))
    return [
        jnp.sum(load(i) * wide, axis=1, keepdims=True) for i in range(width // 8)
    ]


def scatter_products(tiles, place, live, group, columns, slots, width, spread):
    sums = [jnp.zeros((8, width), F32) for _ in range(1, slots)]
    for i, piece in enumerate(columns):
        for slot in range(1, slots):
            part = tiles[group, slot - 1, 8 * i : 8 * i + 8, :] * piece
            sums[slot - 1] = sums[slot - 1] + part
    for slot in range(1, slots):
        where = place[group, slot]
        kept = jnp.where(live[group, slot] > 0, sums[slot - 1], 0.0)
        spread[where, :, :width] = spread[where, :, :width] + kept


def upper_columns(tiles, place, live, wide, group, slots, width):
    rows = []
    for slot in range(1, slots):
        row = wide[place[group, slot], :, :width]
        rows.append(jnp.where(live[group, slot] > 0, row, 0.0))
    pieces = []
    for i in range(width // 8):
        part = tiles[group, 0, 8 * i : 8 * i + 8, :] * rows[0]
        for slot in range(2, slots):
            part = part + tiles[group, slot - 1, 8 * i : 8 * i + 8, :] * rows[slot - 1]
        pieces.append(jnp.sum(part, axis=1, keepdims=True))
    return pieces


def where_am_i(spot):
    return spot[0], spot[1] == 1, spot[2] == 1


def begin_kernel(blocks, slots, width, count,
                 cols_hbm, counts_hbm, right_hbm, jacobi_hbm, tiles_hbm,
                 jacobi, tiles, right, place, live, spot, z, near, one_out, odd_out, back_out, even_out,
                 cols, counts, spread, sems, jacobi_sem, tile_sem):
    small = [
        pltpu.make_async_copy(counts_hbm, counts, sems.at[0]),
        pltpu.make_async_copy(cols_hbm, cols, sems.at[1]),
        pltpu.make_async_copy(right_hbm, right, sems.at[2]),
    ]

    def jacobi_copy(g):
        return pltpu.make_async_copy(jacobi_hbm.at[g], jacobi.at[g], jacobi_sem.at[g])

    def tile_copy(g, k):
        return pltpu.make_async_copy(
            tiles_hbm.at[g, k], tiles.at[g, k - 1], tile_sem.at[g, k - 1]
        )

    for copy in small:
        copy.start()
    for g in range(blocks):
        jacobi_copy(g).start()
    small[0].wait()

    @pl.loop(0, blocks)
    def _(g):
        @pl.loop(1, counts[g])
        def _(k):
            tile_copy(g, k).start()

    @pl.loop(0, blocks)
    def _(g):
        @pl.loop(counts[g], slots)
        def _(k):
            tiles[g, k - 1] = jnp.zeros((width, width), F32)

    small[1].wait()
    base = cols[0, 0]
    me = base // blocks
    spot[0] = me // 2
    spot[1] = me % 2
    spot[2] = (me // 2) % 2
    for g in range(blocks):
        for k in range(slots):
            ahead = cols[g, k] - base
            ahead = jnp.where(ahead < 0, ahead + count * blocks, ahead)
            place[g, k] = jnp.clip(ahead, 0, (BAND + 1) * blocks - 1)
            live[g, k] = (k < counts[g]).astype(jnp.int32)
    spread[...] = jnp.zeros_like(spread)
    small[2].wait()

    for g in range(blocks):
        jacobi_copy(g).wait()
        columns = times_row(
            lambda i: jacobi[g, 8 * i : 8 * i + 8, :], right[g : g + 1, :], width
        )
        z[g : g + 1, :] = columns_to_row(columns, width)

        @pl.loop(1, counts[g])
        def _(k):
            tile_copy(g, k).wait()

        scatter_products(tiles, place, live, g, columns, slots, width, spread)
    sums = jnp.sum(spread[...], axis=1)
    near[...] = sums[:blocks]
    one, two = sums[blocks : 2 * blocks], sums[2 * blocks :]
    _, _, odd = where_am_i(spot)
    rows = z[...]
    one_out[...] = one
    back_out[...] = rows
    odd_out[...] = jnp.where(odd, two, rows)
    even_out[...] = jnp.where(odd, rows, two)


def diagonal_product(blocks, width, diagonal, rows, out):
    for g in range(blocks):
        columns = times_row(
            lambda i: diagonal[g, 8 * i : 8 * i + 8, :], rows[g : g + 1, :], width
        )
        out[g : g + 1, :] = columns_to_row(columns, width)


def first_diagonal_kernel(blocks, width, tiles_hbm, z, near, diagonal, near_out, sem):
    copies = [
        pltpu.make_async_copy(tiles_hbm.at[g, 0], diagonal.at[g], sem.at[g])
        for g in range(blocks)
    ]
    for copy in copies:
        copy.start()
    for copy in copies:
        copy.wait()
    diagonal_product(blocks, width, diagonal, z, near_out)
    near_out[...] = near_out[...] + near[...]


def join_kernel(spot, near, forward_in, odd_in, back_in, even_in, known, one, two):
    _, _, odd = where_am_i(spot)
    one[...] = back_in[...]
    two[...] = jnp.where(odd, odd_in[...], even_in[...])
    known[...] = near[...] + forward_in[...] + jnp.where(odd, even_in[...], odd_in[...])


def spread_rows(wide, rows, first):
    for i in range(rows.shape[0]):
        wide[first + i, :, :] = jnp.broadcast_to(rows[i : i + 1], wide.shape[1:])


def middle_kernel(blocks, slots, width,
                  place, live, tiles, jacobi, z, known, one, two, right,
                  image, swap, far, near, wide, spread):
    lanes = padded(width)
    spread_rows(wide, z[...], 0)
    spread_rows(wide, one[...], blocks)
    spread_rows(wide, two[...], 2 * blocks)
    spread[...] = jnp.zeros_like(spread)
    for g in range(blocks):
        columns = upper_columns(tiles, place, live, wide, g, slots, width)
        image[g : g + 1, :] = known[g : g + 1, :] + columns_to_row(columns, width)
    q = image[...]
    size = jnp.max(jnp.max(jnp.abs(q), axis=1, keepdims=True), axis=0, keepdims=True)
    size = jnp.where(size > TINY, size, 1.0)
    scaled = q * (1.0 / size)
    for g in range(blocks):
        columns = times_row(
            lambda i: jacobi[g, 8 * i : 8 * i + 8, :], scaled[g : g + 1, :], width
        )
        swap[g : g + 1, :] = columns_to_row(columns, width)
        scatter_products(tiles, place, live, g, columns, slots, width, spread)
    sums = jnp.sum(spread[...], axis=1)
    far[...] = sums[2 * blocks :]
    near[...] = sums[:blocks]
    swap[blocks : 2 * blocks, :] = sums[blocks : 2 * blocks]
    values = [size, total(right[...] * z[:, :width]), total(z[...] * q)]
    swap[0:1, :] = swap[0:1, :] + lay_scalars(values, lanes, width)


def second_diagonal_kernel(blocks, width, right, diagonal_tiles, image, swap, near, near_out, out):
    lanes = padded(width)
    keep = iota((blocks, lanes), 1) < width
    w = jnp.where(keep, swap[:blocks, :], 0.0)
    diagonal_product(blocks, width, diagonal_tiles, swap, near_out)
    diagonal = near_out[...]
    values = [
        total(right[...] * w[:, :width]),
        total(image[...] * w),
        total(w * (diagonal + 2.0 * near[...])),
    ]
    near_out[...] = diagonal + near[...]
    out[...] = lay_scalars(values, 128, 0)


def fold(head, other, width, extra):
    tail = width - 256
    lane = iota((head.shape[0], 128), 1)
    last = jnp.where(lane < tail, head[:, 256:384], pltpu.roll(other[:, 256:384], tail, 1))
    last = jnp.where(lane < 2 * tail, last, extra)
    return head[:, :128], head[:, 128:256], other[:, :128], other[:, 128:256], last


def unfold_first(part, width):
    tail = width - 256
    last = jnp.where(iota(part.shape[1:], 1) < tail, part[4], 0.0)
    return jnp.concatenate([part[0], part[1], last], axis=1)


def unfold_second(part, width):
    tail = width - 256
    last = jnp.where(iota(part.shape[1:], 1) < tail, pltpu.roll(part[4], 128 - tail, 1), 0.0)
    return jnp.concatenate([part[2], part[3], last], axis=1)


def gather_kernel(blocks, width, spot, swap, swapped, far, dots, out):
    _, second, _ = where_am_i(spot)
    rows, other = swap[...], swapped[...]

    def at(block, i):
        return block[0:1, width + i : width + i + 1]

    mine, theirs = at(rows, 0), at(other, 0)
    scale = jnp.where(second, mine, jnp.maximum(mine, theirs))
    sent = far[...] * (mine / scale) + jnp.where(
        second, 0.0, other[blocks:] * (theirs / scale)
    )
    crossing = total(rows[blocks:, :width] * other[:blocks, :width])
    values = [
        mine,
        scale,
        at(rows, 1) + at(other, 1),
        at(rows, 2) + at(other, 2),
        dots[0:1, 0:1],
        dots[0:1, 1:2] / mine,
        at(rows, 2),
        dots[0:1, 2:3],
        jnp.where(second, 0.0, 2.0 * crossing),
        theirs,
    ]
    extra = lay_scalars(values, 128, 2 * (width - 256))
    parts = fold(rows[:blocks], sent, width, extra)
    for e in range(out.shape[0]):
        for i, part in enumerate(parts):
            out[e, i] = part


def after_kernel(spot, gathered, out):
    chips = gathered.shape[0]
    chip, _, _ = where_am_i(spot)
    out[...] = gathered[jnp.where(chip == chips - 1, 0, chip + 1)]


def sums_kernel(blocks, width, gathered, out):
    chips = gathered.shape[0]
    tail = width - 256
    table = jnp.concatenate([gathered[e, 4, 0:1, :] for e in range(chips)], axis=0)
    later = jnp.concatenate([table[1:], table[:1]], axis=0)

    def at(i, rows=table):
        return rows[:, 2 * tail + i : 2 * tail + i + 1]

    def chips_total(value):
        return jnp.sum(value, axis=0, keepdims=True)

    norm = chips_total(at(2))
    along = chips_total(at(3))
    alpha = norm / along
    size = alpha * at(0)
    fresh = chips_total(size * (size * at(5) - at(4)) - alpha * at(6))
    diagonal = chips_total(
        size * (size * at(7) + (alpha * at(9)) * at(8) - 2.0 * at(0) * at(5))
    )
    weight = (alpha * at(1)) * (alpha * at(0, later))
    inside = iota((blocks, 128), 1) < tail
    lines = []
    for e in range(chips):
        n = (e + 1) % chips
        ends = jnp.where(inside, pltpu.roll(gathered[e, 4], 128 - tail, 1) * gathered[n, 4], 0.0)
        pair = gathered[e, 2] * gathered[n, 0] + gathered[e, 3] * gathered[n, 1] + ends
        lines.append(jnp.sum(pair, axis=0, keepdims=True))
    edges = total(jnp.concatenate(lines, axis=0) * weight)
    values = [fresh, diagonal + 2.0 * edges, norm, along]
    out[...] = jnp.broadcast_to(lay_scalars(values, 128, 0), out.shape)


def later_kernel(blocks, slots, width,
                 place, live, spot, tiles, swap, swapped, near, gathered, next_part, next_other, sums,
                 product, scaled, wide):
    chips = gathered.shape[0]
    lanes = padded(width)
    chip, second, _ = where_am_i(spot)
    tail = width - 256
    before = gathered[jnp.where(chip == 0, chips - 1, chip - 1)]
    alpha = sums[0:1, 2:3] / sums[0:1, 3:4]

    def at(part, i):
        return alpha * part[4, 0:1, 2 * tail + i : 2 * tail + i + 1]

    mine = alpha * swap[0:1, width : width + 1]
    theirs = alpha * swapped[0:1, width : width + 1]
    keep = iota((blocks, lanes), 1) < width
    w = jnp.where(keep, swap[:blocks, :], 0.0) * mine
    w_other = jnp.where(keep, swapped[:blocks, :], 0.0) * theirs
    ahead, ahead_other = next_part[...], next_other[...]
    ahead = unfold_first(ahead, width) * at(ahead, 0)
    ahead_other = unfold_first(ahead_other, width) * at(ahead_other, 0)
    scaled[...] = w
    spread_rows(wide, w, 0)
    spread_rows(wide, jnp.where(second, ahead_other, w_other), blocks)
    spread_rows(wide, ahead, 2 * blocks)
    known = near[...] * mine + unfold_second(before, width) * at(before, 1)
    product[...] = known + jnp.where(second, swapped[blocks:, :] * theirs, 0.0)

    for g in range(blocks):
        columns = upper_columns(tiles, place, live, wide, g, slots, width)
        product[g : g + 1, :] = product[g : g + 1, :] + columns_to_row(columns, width)


def end_kernel(blocks, width, right, z_ref, image, product, scaled, sums, sums_other,
               update, residual):
    def shared(i):
        return sums[0:1, i : i + 1] + sums_other[0:1, i : i + 1]

    norm, along = sums[0:1, 2:3], sums[0:1, 3:4]
    alpha = norm / along
    fresh = norm + shared(0)
    curved = along + shared(1)
    ratio = fresh / norm
    step = fresh / (curved - ratio * (fresh / alpha))
    z, q = z_ref[...], image[...]
    z_next = z - scaled[...]
    update[...] = (alpha * z + step * (z_next + ratio * z))[:, :width]
    r_next = right[...] - (alpha * q)[:, :width]
    residual[...] = r_next - (step * ((q - product[...]) + ratio * q))[:, :width]


def on_device(right_side, schur_tiles, block_cols, tile_counts, jacobi_inverse):
    count = lax.axis_size(AXIS)
    blocks, slots, width, _ = schur_tiles.shape
    lanes = padded(width)
    chips = count // 2
    vmem = pl.BlockSpec(memory_space=pltpu.VMEM)
    smem = pl.BlockSpec(memory_space=pltpu.SMEM)
    hbm = pl.BlockSpec(memory_space=pltpu.HBM)
    rows = pltpu.VMEM((2 * blocks, lanes), F32)
    half = pltpu.VMEM((blocks, lanes), F32)
    small = pltpu.VMEM((8, 128), F32)
    spread = pltpu.VMEM(((BAND + 1) * blocks, 8, lanes), F32)
    index = pltpu.SMEM((blocks, slots), jnp.int32)

    def call(kernel, sizes, in_specs, out_shape, scratch=(), work=0):
        single = not isinstance(out_shape, list)
        shapes = [out_shape] if single else out_shape
        specs = [
            smem if getattr(shape, "memory_space", None) == pltpu.SMEM else vmem
            for shape in shapes
        ]
        return pl.pallas_call(
            functools.partial(kernel, *sizes),
            in_specs=in_specs,
            out_specs=specs[0] if single else specs,
            out_shape=out_shape,
            scratch_shapes=list(scratch),
            compiler_params=pltpu.CompilerParams(vmem_limit_bytes=VMEM_LIMIT),
            cost_estimate=pl.CostEstimate(
                flops=2 * work * width * width, bytes_accessed=4 * work * width * width, transcendentals=0
            ),
        )

    def swap_cores(value):
        return lax.ppermute(value, AXIS, [(i, i ^ 1) for i in range(count)])

    def swap_chips(odd, value):
        pairs = []
        for i in range(count):
            chip, core = divmod(i, 2)
            step = 1 if (chip % 2 == 1) == odd else -1
            pairs.append((i, 2 * ((chip + step) % chips) + core))
        return lax.ppermute(value, AXIS, pairs)

    sizes = (blocks, slots, width)
    off_chip = [
        pltpu.with_memory_space_constraint(value, pltpu.HBM)
        for value in (block_cols, tile_counts, right_side, jacobi_inverse, schur_tiles)
    ]
    jacobi, tiles, right, place, live, spot, z, near, one_out, odd_out, back_out, even_out = call(
        begin_kernel, sizes + (count,), [hbm] * 5,
        [
            pltpu.VMEM(jacobi_inverse.shape, F32),
            pltpu.VMEM((blocks, slots - 1, width, width), F32),
            pltpu.VMEM(right_side.shape, F32),
            index, index, pltpu.SMEM((4,), jnp.int32),
            half, half, half, half, half, half,
        ],
        [
            pltpu.SMEM(block_cols.shape, jnp.int32),
            pltpu.SMEM(tile_counts.shape, jnp.int32),
            spread,
            pltpu.SemaphoreType.DMA((3,)),
            pltpu.SemaphoreType.DMA((blocks,)),
            pltpu.SemaphoreType.DMA((blocks, slots - 1)),
        ],
        work=blocks * slots,
    )(*off_chip)
    forward_in = lax.ppermute(one_out, AXIS, [(i, (i + 1) % count) for i in range(count)])
    odd_in = swap_chips(True, odd_out)
    back_in = lax.ppermute(back_out, AXIS, [((i + 1) % count, i) for i in range(count)])
    even_in = swap_chips(False, even_out)
    diagonal, near1 = call(
        first_diagonal_kernel, (blocks, width), [hbm, vmem, vmem],
        [pltpu.VMEM((blocks, width, width), F32), half],
        [pltpu.SemaphoreType.DMA((blocks,))],
        work=blocks,
    )(off_chip[4], z, near)
    known, one, two = call(join_kernel, (), [smem] + [vmem] * 5, [half, half, half])(
        spot, near1, forward_in, odd_in, back_in, even_in
    )
    image, swap, far, near2 = call(
        middle_kernel, sizes, [smem] * 2 + [vmem] * 7, [half, rows, half, half], [spread, spread],
        work=3 * blocks * slots,
    )(place, live, tiles, jacobi, z, known, one, two, right)
    swapped = swap_cores(swap)
    near3, dots = call(
        second_diagonal_kernel, (blocks, width), [vmem] * 5, [half, pltpu.VMEM((1, 128), F32)], work=blocks
    )(right, diagonal, image, swap, near2)
    sent = call(
        gather_kernel, (blocks, width), [smem] + [vmem] * 4, pltpu.VMEM((chips, 5, blocks, 128), F32)
    )(spot, swap, swapped, far, dots)
    groups = [[2 * c + core for c in range(chips)] for core in range(2)]
    gathered = lax.all_to_all(sent, AXIS, 0, 0, axis_index_groups=groups)
    next_part = call(after_kernel, (), [smem, vmem], pltpu.VMEM((5, blocks, 128), F32))(spot, gathered)
    next_other = swap_cores(next_part)
    sums = call(sums_kernel, (blocks, width), [vmem], small, work=chips)(gathered)
    sums_other = swap_cores(sums)
    product, scaled = call(
        later_kernel, sizes, [smem] * 3 + [vmem] * 8, [half, half], [spread], work=blocks * slots,
    )(place, live, spot, tiles, swap, swapped, near3, gathered, next_part, next_other, sums)
    out = jax.ShapeDtypeStruct(right_side.shape, F32)
    return call(end_kernel, (blocks, width), [vmem] * 7, [out, out])(
        right, z, image, product, scaled, sums, sums_other
    )


def solution(mesh):
    placed = (
        P(AXIS, None),
        P(AXIS, None, None, None),
        P(AXIS, None),
        P(AXIS),
        P(AXIS, None, None),
    )
    return jax.shard_map(
        on_device,
        mesh=mesh,
        in_specs=placed,
        out_specs=(P(AXIS, None), P(AXIS, None)),
        check_vma=False,
    )
```

```python
import functools

import jax
import jax.numpy as jnp
from jax import lax
from jax.experimental import pallas as pl
from jax.experimental.pallas import tpu as pltpu
from jax.sharding import PartitionSpec as P

AXIS = "cams"
BAND = 2
F32 = jnp.float32
VMEM_LIMIT = 40 * 2**20
TINY = 1e-30


def padded(width):
    return -(-width // 128) * 128


def iota(shape, dim):
    return lax.broadcasted_iota(jnp.int32, shape, dim)


def total(value):
    return jnp.sum(jnp.sum(value, axis=1, keepdims=True), axis=0, keepdims=True)


def lay_scalars(values, lanes, first):
    lane = iota((1, lanes), 1)
    row = jnp.zeros((1, lanes), F32)
    for i, value in enumerate(values):
        row = jnp.where(lane == first + i, value, row)
    return row


def columns_to_row(columns, width):
    lanes = padded(width)
    skew = iota((8, 128), 1) - iota((8, 128), 0)
    parts = [jnp.zeros((8, 128), F32) for _ in range(lanes // 128)]
    for i, piece in enumerate(columns):
        tile, lane = divmod(8 * i, 128)
        parts[tile] = parts[tile] + jnp.where(skew == lane, piece, 0.0)
    return jnp.sum(jnp.concatenate(parts, axis=1), axis=0, keepdims=True)


def times_row(load, row, width):
    wide = jnp.broadcast_to(row[:, :width], (8, width))
    return [
        jnp.sum(load(i) * wide, axis=1, keepdims=True) for i in range(width // 8)
    ]


def scatter_products(tiles, place, live, group, columns, slots, width, spread):
    sums = [jnp.zeros((8, width), F32) for _ in range(1, slots)]
    for i, piece in enumerate(columns):
        for slot in range(1, slots):
            part = tiles[group, slot - 1, 8 * i : 8 * i + 8, :] * piece
            sums[slot - 1] = sums[slot - 1] + part
    for slot in range(1, slots):
        where = place[group, slot]
        kept = jnp.where(live[group, slot] > 0, sums[slot - 1], 0.0)
        spread[where, :, :width] = spread[where, :, :width] + kept


def upper_columns(tiles, place, live, wide, group, slots, width):
    rows = []
    for slot in range(1, slots):
        row = wide[place[group, slot], :, :width]
        rows.append(jnp.where(live[group, slot] > 0, row, 0.0))
    pieces = []
    for i in range(width // 8):
        part = tiles[group, 0, 8 * i : 8 * i + 8, :] * rows[0]
        for slot in range(2, slots):
            part = part + tiles[group, slot - 1, 8 * i : 8 * i + 8, :] * rows[slot - 1]
        pieces.append(jnp.sum(part, axis=1, keepdims=True))
    return pieces


def where_am_i(spot):
    return spot[0], spot[1] == 1, spot[2] == 1


def begin_kernel(blocks, slots, width, count,
                 cols_hbm, counts_hbm, right_hbm, jacobi_hbm, tiles_hbm,
                 jacobi, tiles, right, place, live, spot, z, near, one_out, odd_out, back_out, even_out,
                 cols, counts, spread, sems, jacobi_sem, tile_sem):
    small = [
        pltpu.make_async_copy(counts_hbm, counts, sems.at[0]),
        pltpu.make_async_copy(cols_hbm, cols, sems.at[1]),
        pltpu.make_async_copy(right_hbm, right, sems.at[2]),
    ]

    def jacobi_copy(g):
        return pltpu.make_async_copy(jacobi_hbm.at[g], jacobi.at[g], jacobi_sem.at[g])

    def tile_copy(g, k):
        return pltpu.make_async_copy(
            tiles_hbm.at[g, k], tiles.at[g, k - 1], tile_sem.at[g, k - 1]
        )

    for copy in small:
        copy.start()
    for g in range(blocks):
        jacobi_copy(g).start()
    small[0].wait()

    @pl.loop(0, blocks)
    def _(g):
        @pl.loop(1, counts[g])
        def _(k):
            tile_copy(g, k).start()

    @pl.loop(0, blocks)
    def _(g):
        @pl.loop(counts[g], slots)
        def _(k):
            tiles[g, k - 1] = jnp.zeros((width, width), F32)

    small[1].wait()
    base = cols[0, 0]
    me = base // blocks
    spot[0] = me // 2
    spot[1] = me % 2
    spot[2] = (me // 2) % 2
    for g in range(blocks):
        for k in range(slots):
            ahead = cols[g, k] - base
            ahead = jnp.where(ahead < 0, ahead + count * blocks, ahead)
            place[g, k] = jnp.clip(ahead, 0, (BAND + 1) * blocks - 1)
            live[g, k] = (k < counts[g]).astype(jnp.int32)
    spread[...] = jnp.zeros_like(spread)
    small[2].wait()

    for g in range(blocks):
        jacobi_copy(g).wait()
        columns = times_row(
            lambda i: jacobi[g, 8 * i : 8 * i + 8, :], right[g : g + 1, :], width
        )
        z[g : g + 1, :] = columns_to_row(columns, width)

        @pl.loop(1, counts[g])
        def _(k):
            tile_copy(g, k).wait()

        scatter_products(tiles, place, live, g, columns, slots, width, spread)
    sums = jnp.sum(spread[...], axis=1)
    near[...] = sums[:blocks]
    one, two = sums[blocks : 2 * blocks], sums[2 * blocks :]
    _, _, odd = where_am_i(spot)
    rows = z[...]
    one_out[...] = one
    back_out[...] = rows
    odd_out[...] = jnp.where(odd, two, rows)
    even_out[...] = jnp.where(odd, rows, two)


def diagonal_product(blocks, width, diagonal, rows, out):
    for g in range(blocks):
        columns = times_row(
            lambda i: diagonal[g, 8 * i : 8 * i + 8, :], rows[g : g + 1, :], width
        )
        out[g : g + 1, :] = columns_to_row(columns, width)


def first_diagonal_kernel(blocks, width, tiles_hbm, z, near, diagonal, near_out, sem):
    copies = [
        pltpu.make_async_copy(tiles_hbm.at[g, 0], diagonal.at[g], sem.at[g])
        for g in range(blocks)
    ]
    for copy in copies:
        copy.start()
    for copy in copies:
        copy.wait()
    diagonal_product(blocks, width, diagonal, z, near_out)
    near_out[...] = near_out[...] + near[...]


def join_kernel(spot, near, forward_in, odd_in, back_in, even_in, known, one, two):
    _, _, odd = where_am_i(spot)
    one[...] = back_in[...]
    two[...] = jnp.where(odd, odd_in[...], even_in[...])
    known[...] = near[...] + forward_in[...] + jnp.where(odd, even_in[...], odd_in[...])


def spread_rows(wide, rows, first):
    for i in range(rows.shape[0]):
        wide[first + i, :, :] = jnp.broadcast_to(rows[i : i + 1], wide.shape[1:])


def middle_kernel(blocks, slots, width,
                  place, live, tiles, jacobi, z, known, one, two, right,
                  image, swap, far, near, wide, spread):
    lanes = padded(width)
    spread_rows(wide, z[...], 0)
    spread_rows(wide, one[...], blocks)
    spread_rows(wide, two[...], 2 * blocks)
    spread[...] = jnp.zeros_like(spread)
    for g in range(blocks):
        columns = upper_columns(tiles, place, live, wide, g, slots, width)
        image[g : g + 1, :] = known[g : g + 1, :] + columns_to_row(columns, width)
    q = image[...]
    size = jnp.max(jnp.max(jnp.abs(q), axis=1, keepdims=True), axis=0, keepdims=True)
    size = jnp.where(size > TINY, size, 1.0)
    scaled = q * (1.0 / size)
    for g in range(blocks):
        columns = times_row(
            lambda i: jacobi[g, 8 * i : 8 * i + 8, :], scaled[g : g + 1, :], width
        )
        swap[g : g + 1, :] = columns_to_row(columns, width)
        scatter_products(tiles, place, live, g, columns, slots, width, spread)
    sums = jnp.sum(spread[...], axis=1)
    far[...] = sums[2 * blocks :]
    near[...] = sums[:blocks]
    swap[blocks : 2 * blocks, :] = sums[blocks : 2 * blocks]
    values = [size, total(right[...] * z[:, :width]), total(z[...] * q)]
    for i, value in enumerate(values):
        swap[2 * blocks + i : 2 * blocks + i + 1, :] = jnp.broadcast_to(value, (1, lanes))


def second_diagonal_kernel(blocks, width, right, diagonal_tiles, image, swap, near, near_out, out):
    w = swap[:blocks, :]
    diagonal_product(blocks, width, diagonal_tiles, swap, near_out)
    diagonal = near_out[...]
    values = [
        total(right[...] * w[:, :width]),
        total(image[...] * w),
        total(w * (diagonal + 2.0 * near[...])),
    ]
    near_out[...] = diagonal + near[...]
    out[...] = lay_scalars(values, 128, 0)


def fold(head, other, width, extra):
    tail = width - 256
    lane = iota((head.shape[0], 128), 1)
    last = jnp.where(lane < tail, head[:, 256:384], pltpu.roll(other[:, 256:384], tail, 1))
    last = jnp.where(lane < 2 * tail, last, extra)
    return head[:, :128], head[:, 128:256], other[:, :128], other[:, 128:256], last


def unfold_first(part, width):
    tail = width - 256
    last = jnp.where(iota(part.shape[1:], 1) < tail, part[4], 0.0)
    return jnp.concatenate([part[0], part[1], last], axis=1)


def unfold_second(part, width):
    tail = width - 256
    last = jnp.where(iota(part.shape[1:], 1) < tail, pltpu.roll(part[4], 128 - tail, 1), 0.0)
    return jnp.concatenate([part[2], part[3], last], axis=1)


def gather_kernel(blocks, width, spot, swap, swapped, far, dots, out):
    _, second, _ = where_am_i(spot)
    rows, other = swap[...], swapped[...]

    def at(block, i):
        return block[2 * blocks + i : 2 * blocks + i + 1]

    mine, theirs = at(rows, 0), at(other, 0)
    scale = jnp.where(second, mine, jnp.maximum(mine, theirs))
    sent = far[...] * (mine / scale) + jnp.where(
        second, 0.0, other[blocks : 2 * blocks] * (theirs / scale)
    )
    crossing = total(rows[blocks : 2 * blocks] * other[:blocks])
    values = [
        mine[:, :128],
        scale[:, :128],
        (at(rows, 1) + at(other, 1))[:, :128],
        (at(rows, 2) + at(other, 2))[:, :128],
        dots[0:1, 0:1],
        dots[0:1, 1:2] / mine[:, :1],
        at(rows, 2)[:, :128],
        dots[0:1, 2:3],
        jnp.where(second, 0.0, 2.0 * crossing),
        theirs[:, :128],
    ]
    extra = lay_scalars(values, 128, 2 * (width - 256))
    parts = fold(rows[:blocks], sent, width, extra)
    for e in range(out.shape[0]):
        for i, part in enumerate(parts):
            out[e, i] = part


def after_kernel(spot, gathered, out):
    chips = gathered.shape[0]
    chip, _, _ = where_am_i(spot)
    out[...] = gathered[jnp.where(chip == chips - 1, 0, chip + 1)]


def sums_kernel(blocks, width, gathered, out):
    chips = gathered.shape[0]
    tail = width - 256
    table = jnp.concatenate([gathered[e, 4, 0:1, :] for e in range(chips)], axis=0)
    later = jnp.concatenate([table[1:], table[:1]], axis=0)

    def at(i, rows=table):
        return rows[:, 2 * tail + i : 2 * tail + i + 1]

    def chips_total(value):
        return jnp.sum(value, axis=0, keepdims=True)

    norm = chips_total(at(2))
    along = chips_total(at(3))
    alpha = norm / along
    size = alpha * at(0)
    fresh = chips_total(size * (size * at(5) - at(4)) - alpha * at(6))
    diagonal = chips_total(
        size * (size * at(7) + (alpha * at(9)) * at(8) - 2.0 * at(0) * at(5))
    )
    weight = (alpha * at(1)) * (alpha * at(0, later))
    inside = iota((blocks, 128), 1) < tail
    lines = []
    for e in range(chips):
        n = (e + 1) % chips
        ends = jnp.where(inside, pltpu.roll(gathered[e, 4], 128 - tail, 1) * gathered[n, 4], 0.0)
        pair = gathered[e, 2] * gathered[n, 0] + gathered[e, 3] * gathered[n, 1] + ends
        lines.append(jnp.sum(pair, axis=0, keepdims=True))
    edges = total(jnp.concatenate(lines, axis=0) * weight)
    values = [fresh, diagonal + 2.0 * edges, norm, along, alpha, 1.0 / norm, along / norm]
    for i, value in enumerate(values):
        out[i : i + 1, :] = jnp.broadcast_to(value, (1, out.shape[1]))


def prepare_kernel(blocks, width, spot, swap, swapped, near, gathered, next_part, sums,
                   known, scaled, factor, wide):
    chips = gathered.shape[0]
    chip, second, _ = where_am_i(spot)
    tail = width - 256
    before = gathered[jnp.where(chip == 0, chips - 1, chip - 1)]
    ahead = next_part[...]
    alpha = sums[4:5, :]

    def at(part, i):
        return alpha * part[4, 0:1, 2 * tail + i : 2 * tail + i + 1]

    mine = alpha * swap[2 * blocks : 2 * blocks + 1, :]
    theirs = alpha * swapped[2 * blocks : 2 * blocks + 1, :]
    w = swap[:blocks, :] * mine
    scaled[...] = w
    factor[...] = at(ahead, 9)
    spread_rows(wide, w, 0)
    spread_rows(wide, swapped[:blocks, :] * theirs, blocks)
    spread_rows(wide, unfold_first(ahead, width) * at(ahead, 0), 2 * blocks)
    here = near[...] * mine + unfold_second(before, width) * at(before, 1)
    known[...] = here + jnp.where(second, swapped[blocks : 2 * blocks, :] * theirs, 0.0)


def later_kernel(blocks, slots, width,
                 place, live, spot, tiles, known, factor, ready, next_other,
                 product, wide):
    _, second, _ = where_am_i(spot)
    wide[...] = ready[...]

    @pl.when(second)
    def _():
        spread_rows(wide, unfold_first(next_other[...], width) * factor[...], blocks)

    for g in range(blocks):
        columns = upper_columns(tiles, place, live, wide, g, slots, width)
        product[g : g + 1, :] = known[g : g + 1, :] + columns_to_row(columns, width)


def end_kernel(blocks, width, right, z_ref, image, product, scaled, sums, sums_other,
               update, residual):
    norm, along = sums[2:3, :], sums[3:4, :]
    alpha = sums[4:5, :]
    fresh = norm + (sums[0:1, :] + sums_other[0:1, :])
    curved = along + (sums[1:2, :] + sums_other[1:2, :])
    ratio = fresh * sums[5:6, :]
    step = fresh / (curved - ratio * (fresh * sums[6:7, :]))
    z, q = z_ref[...], image[...]
    z_next = z - scaled[...]
    update[...] = (alpha * z + step * (z_next + ratio * z))[:, :width]
    r_next = right[...] - (alpha * q)[:, :width]
    residual[...] = r_next - (step * ((q - product[...]) + ratio * q))[:, :width]


def on_device(right_side, schur_tiles, block_cols, tile_counts, jacobi_inverse):
    count = lax.axis_size(AXIS)
    blocks, slots, width, _ = schur_tiles.shape
    lanes = padded(width)
    chips = count // 2
    vmem = pl.BlockSpec(memory_space=pltpu.VMEM)
    smem = pl.BlockSpec(memory_space=pltpu.SMEM)
    hbm = pl.BlockSpec(memory_space=pltpu.HBM)
    rows = pltpu.VMEM((2 * blocks, lanes), F32)
    half = pltpu.VMEM((blocks, lanes), F32)
    small = pltpu.VMEM((8, lanes), F32)
    more = pltpu.VMEM((4 * blocks, lanes), F32)
    spread = pltpu.VMEM(((BAND + 1) * blocks, 8, lanes), F32)
    index = pltpu.SMEM((blocks, slots), jnp.int32)

    def call(kernel, sizes, in_specs, out_shape, scratch=(), work=0):
        single = not isinstance(out_shape, list)
        shapes = [out_shape] if single else out_shape
        specs = [
            smem if getattr(shape, "memory_space", None) == pltpu.SMEM else vmem
            for shape in shapes
        ]
        return pl.pallas_call(
            functools.partial(kernel, *sizes),
            in_specs=in_specs,
            out_specs=specs[0] if single else specs,
            out_shape=out_shape,
            scratch_shapes=list(scratch),
            compiler_params=pltpu.CompilerParams(vmem_limit_bytes=VMEM_LIMIT),
            cost_estimate=pl.CostEstimate(
                flops=2 * work * width * width, bytes_accessed=4 * work * width * width, transcendentals=0
            ),
        )

    def swap_cores(value):
        return lax.ppermute(value, AXIS, [(i, i ^ 1) for i in range(count)])

    def swap_chips(odd, value):
        pairs = []
        for i in range(count):
            chip, core = divmod(i, 2)
            step = 1 if (chip % 2 == 1) == odd else -1
            pairs.append((i, 2 * ((chip + step) % chips) + core))
        return lax.ppermute(value, AXIS, pairs)

    sizes = (blocks, slots, width)
    off_chip = [
        pltpu.with_memory_space_constraint(value, pltpu.HBM)
        for value in (block_cols, tile_counts, right_side, jacobi_inverse, schur_tiles)
    ]
    jacobi, tiles, right, place, live, spot, z, near, one_out, odd_out, back_out, even_out = call(
        begin_kernel, sizes + (count,), [hbm] * 5,
        [
            pltpu.VMEM(jacobi_inverse.shape, F32),
            pltpu.VMEM((blocks, slots - 1, width, width), F32),
            pltpu.VMEM(right_side.shape, F32),
            index, index, pltpu.SMEM((4,), jnp.int32),
            half, half, half, half, half, half,
        ],
        [
            pltpu.SMEM(block_cols.shape, jnp.int32),
            pltpu.SMEM(tile_counts.shape, jnp.int32),
            spread,
            pltpu.SemaphoreType.DMA((3,)),
            pltpu.SemaphoreType.DMA((blocks,)),
            pltpu.SemaphoreType.DMA((blocks, slots - 1)),
        ],
        work=blocks * slots,
    )(*off_chip)
    forward_in = lax.ppermute(one_out, AXIS, [(i, (i + 1) % count) for i in range(count)])
    odd_in = swap_chips(True, odd_out)
    back_in = lax.ppermute(back_out, AXIS, [((i + 1) % count, i) for i in range(count)])
    even_in = swap_chips(False, even_out)
    diagonal, near1 = call(
        first_diagonal_kernel, (blocks, width), [hbm, vmem, vmem],
        [pltpu.VMEM((blocks, width, width), F32), half],
        [pltpu.SemaphoreType.DMA((blocks,))],
        work=blocks,
    )(off_chip[4], z, near)
    known, one, two = call(join_kernel, (), [smem] + [vmem] * 5, [half, half, half])(
        spot, near1, forward_in, odd_in, back_in, even_in
    )
    image, swap, far, near2 = call(
        middle_kernel, sizes, [smem] * 2 + [vmem] * 7, [half, more, half, half], [spread, spread],
        work=3 * blocks * slots,
    )(place, live, tiles, jacobi, z, known, one, two, right)
    swapped = swap_cores(swap)
    near3, dots = call(
        second_diagonal_kernel, (blocks, width), [vmem] * 5, [half, pltpu.VMEM((1, 128), F32)], work=blocks
    )(right, diagonal, image, swap, near2)
    sent = call(
        gather_kernel, (blocks, width), [smem] + [vmem] * 4, pltpu.VMEM((chips, 5, blocks, 128), F32)
    )(spot, swap, swapped, far, dots)
    groups = [[2 * c + core for c in range(chips)] for core in range(2)]
    gathered = lax.all_to_all(sent, AXIS, 0, 0, axis_index_groups=groups)
    next_part = call(after_kernel, (), [smem, vmem], pltpu.VMEM((5, blocks, 128), F32))(spot, gathered)
    next_other = swap_cores(next_part)
    sums = call(sums_kernel, (blocks, width), [vmem], small, work=chips)(gathered)
    sums_other = swap_cores(sums)
    known2, scaled, factor, ready = call(
        prepare_kernel, (blocks, width), [smem] + [vmem] * 6,
        [half, half, pltpu.VMEM((1, lanes), F32), spread],
    )(spot, swap, swapped, near3, gathered, next_part, sums)
    product = call(
        later_kernel, sizes, [smem] * 3 + [vmem] * 5, half, [spread], work=100 * blocks * slots,
    )(place, live, spot, tiles, known2, factor, ready, next_other)
    out = jax.ShapeDtypeStruct(right_side.shape, F32)
    return call(end_kernel, (blocks, width), [vmem] * 7, [out, out])(
        right, z, image, product, scaled, sums, sums_other
    )


def solution(mesh):
    placed = (
        P(AXIS, None),
        P(AXIS, None, None, None),
        P(AXIS, None),
        P(AXIS),
        P(AXIS, None, None),
    )
    return jax.shard_map(
        on_device,
        mesh=mesh,
        in_specs=placed,
        out_specs=(P(AXIS, None), P(AXIS, None)),
        check_vma=False,
    )
```

```python
import functools

import jax
import jax.numpy as jnp
from jax import lax
from jax.experimental import pallas as pl
from jax.experimental.pallas import tpu as pltpu
from jax.sharding import PartitionSpec as P

AXIS = "cams"
BAND = 2
F32 = jnp.float32
VMEM_LIMIT = 40 * 2**20
TINY = 1e-30


def padded(width):
    return -(-width // 128) * 128


def iota(shape, dim):
    return lax.broadcasted_iota(jnp.int32, shape, dim)


def total(value):
    return jnp.sum(jnp.sum(value, axis=1, keepdims=True), axis=0, keepdims=True)


def lay_scalars(values, lanes, first):
    lane = iota((1, lanes), 1)
    row = jnp.zeros((1, lanes), F32)
    for i, value in enumerate(values):
        row = jnp.where(lane == first + i, value, row)
    return row


def columns_to_row(columns, width):
    lanes = padded(width)
    skew = iota((8, 128), 1) - iota((8, 128), 0)
    parts = [jnp.zeros((8, 128), F32) for _ in range(lanes // 128)]
    for i, piece in enumerate(columns):
        tile, lane = divmod(8 * i, 128)
        parts[tile] = parts[tile] + jnp.where(skew == lane, piece, 0.0)
    return jnp.sum(jnp.concatenate(parts, axis=1), axis=0, keepdims=True)


def times_row(load, row, width):
    wide = jnp.broadcast_to(row[:, :width], (8, width))
    return [
        jnp.sum(load(i) * wide, axis=1, keepdims=True) for i in range(width // 8)
    ]


def scatter_products(tiles, place, live, group, columns, slots, width, spread):
    sums = [jnp.zeros((8, width), F32) for _ in range(1, slots)]
    for i, piece in enumerate(columns):
        for slot in range(1, slots):
            part = tiles[group, slot - 1, 8 * i : 8 * i + 8, :] * piece
            sums[slot - 1] = sums[slot - 1] + part
    for slot in range(1, slots):
        where = place[group, slot]
        kept = jnp.where(live[group, slot] > 0, sums[slot - 1], 0.0)
        spread[where, :, :width] = spread[where, :, :width] + kept


def upper_columns(tiles, place, live, wide, group, slots, width):
    rows = []
    for slot in range(1, slots):
        row = wide[place[group, slot], :, :width]
        rows.append(jnp.where(live[group, slot] > 0, row, 0.0))
    pieces = []
    for i in range(width // 8):
        part = tiles[group, 0, 8 * i : 8 * i + 8, :] * rows[0]
        for slot in range(2, slots):
            part = part + tiles[group, slot - 1, 8 * i : 8 * i + 8, :] * rows[slot - 1]
        pieces.append(jnp.sum(part, axis=1, keepdims=True))
    return pieces


def where_am_i(spot):
    return spot[0], spot[1] == 1, spot[2] == 1


def begin_kernel(blocks, slots, width, count,
                 cols_hbm, counts_hbm, right_hbm, jacobi_hbm, tiles_hbm,
                 jacobi, tiles, right, place, live, spot, z, near, one_out, odd_out, back_out, even_out,
                 cols, counts, spread, sems, jacobi_sem, tile_sem):
    small = [
        pltpu.make_async_copy(counts_hbm, counts, sems.at[0]),
        pltpu.make_async_copy(cols_hbm, cols, sems.at[1]),
        pltpu.make_async_copy(right_hbm, right, sems.at[2]),
    ]

    def jacobi_copy(g):
        return pltpu.make_async_copy(jacobi_hbm.at[g], jacobi.at[g], jacobi_sem.at[g])

    def tile_copy(g, k):
        return pltpu.make_async_copy(
            tiles_hbm.at[g, k], tiles.at[g, k - 1], tile_sem.at[g, k - 1]
        )

    for copy in small:
        copy.start()
    for g in range(blocks):
        jacobi_copy(g).start()
    small[0].wait()

    @pl.loop(0, blocks)
    def _(g):
        @pl.loop(1, counts[g])
        def _(k):
            tile_copy(g, k).start()

    @pl.loop(0, blocks)
    def _(g):
        @pl.loop(counts[g], slots)
        def _(k):
            tiles[g, k - 1] = jnp.zeros((width, width), F32)

    small[1].wait()
    base = cols[0, 0]
    me = base // blocks
    spot[0] = me // 2
    spot[1] = me % 2
    spot[2] = (me // 2) % 2
    for g in range(blocks):
        for k in range(slots):
            ahead = cols[g, k] - base
            ahead = jnp.where(ahead < 0, ahead + count * blocks, ahead)
            place[g, k] = jnp.clip(ahead, 0, (BAND + 1) * blocks - 1)
            live[g, k] = (k < counts[g]).astype(jnp.int32)
    spread[...] = jnp.zeros_like(spread)
    small[2].wait()

    every = []
    for g in range(blocks):
        jacobi_copy(g).wait()
        columns = times_row(
            lambda i: jacobi[g, 8 * i : 8 * i + 8, :], right[g : g + 1, :], width
        )
        z[g : g + 1, :] = columns_to_row(columns, width)
        every.append(columns)
    for g in range(blocks):
        columns = every[g]

        @pl.loop(1, counts[g])
        def _(k):
            tile_copy(g, k).wait()

        scatter_products(tiles, place, live, g, columns, slots, width, spread)
    near[...] = spread[:blocks]
    sums = jnp.sum(spread[blocks:], axis=1)
    one, two = sums[:blocks], sums[blocks:]
    _, _, odd = where_am_i(spot)
    rows = z[...]
    one_out[...] = one
    back_out[...] = rows
    odd_out[...] = jnp.where(odd, two, rows)
    even_out[...] = jnp.where(odd, rows, two)


def diagonal_product(blocks, width, diagonal, rows, out):
    for g in range(blocks):
        columns = times_row(
            lambda i: diagonal[g, 8 * i : 8 * i + 8, :], rows[g : g + 1, :], width
        )
        out[g : g + 1, :] = columns_to_row(columns, width)


def first_diagonal_kernel(blocks, width, tiles_hbm, z, near, diagonal, near_out, sem):
    copies = [
        pltpu.make_async_copy(tiles_hbm.at[g, 0], diagonal.at[g], sem.at[g])
        for g in range(blocks)
    ]
    for copy in copies:
        copy.start()
    for copy in copies:
        copy.wait()
    diagonal_product(blocks, width, diagonal, z, near_out)
    near_out[...] = near_out[...] + jnp.sum(near[...], axis=1)


def join_kernel(spot, near, forward_in, odd_in, back_in, even_in, known, one, two):
    _, _, odd = where_am_i(spot)
    one[...] = back_in[...]
    two[...] = jnp.where(odd, odd_in[...], even_in[...])
    known[...] = near[...] + forward_in[...] + jnp.where(odd, even_in[...], odd_in[...])


def spread_rows(wide, rows, first):
    for i in range(rows.shape[0]):
        wide[first + i, :, :] = jnp.broadcast_to(rows[i : i + 1], wide.shape[1:])


def middle_kernel(blocks, slots, width,
                  place, live, tiles, jacobi, z, known, one, two, right,
                  image, swap, far, near, wide, spread):
    lanes = padded(width)
    spread_rows(wide, z[...], 0)
    spread_rows(wide, one[...], blocks)
    spread_rows(wide, two[...], 2 * blocks)
    spread[...] = jnp.zeros_like(spread)
    for g in range(blocks):
        columns = upper_columns(tiles, place, live, wide, g, slots, width)
        image[g : g + 1, :] = known[g : g + 1, :] + columns_to_row(columns, width)
    q = image[...]
    size = jnp.max(jnp.max(jnp.abs(q), axis=1, keepdims=True), axis=0, keepdims=True)
    size = jnp.where(size > TINY, size, 1.0)
    scaled = q * (1.0 / size)
    for g in range(blocks):
        columns = times_row(
            lambda i: jacobi[g, 8 * i : 8 * i + 8, :], scaled[g : g + 1, :], width
        )
        swap[g : g + 1, :] = columns_to_row(columns, width)
        scatter_products(tiles, place, live, g, columns, slots, width, spread)
    sums = jnp.sum(spread[...], axis=1)
    far[...] = sums[2 * blocks :]
    near[...] = sums[:blocks]
    swap[blocks : 2 * blocks, :] = sums[blocks : 2 * blocks]
    values = [size, total(right[...] * z[:, :width]), total(z[...] * q)]
    for i, value in enumerate(values):
        swap[2 * blocks + i : 2 * blocks + i + 1, :] = jnp.broadcast_to(value, (1, lanes))


def second_diagonal_kernel(blocks, width, right, diagonal_tiles, image, swap, near, near_out, out):
    w = swap[:blocks, :]
    diagonal_product(blocks, width, diagonal_tiles, swap, near_out)
    diagonal = near_out[...]
    values = [
        total(right[...] * w[:, :width]),
        total(image[...] * w),
        total(w * (diagonal + 2.0 * near[...])),
    ]
    near_out[...] = diagonal + near[...]
    out[...] = lay_scalars(values, 128, 0)


def fold(head, other, width, extra):
    tail = width - 256
    lane = iota((head.shape[0], 128), 1)
    last = jnp.where(lane < tail, head[:, 256:384], pltpu.roll(other[:, 256:384], tail, 1))
    last = jnp.where(lane < 2 * tail, last, extra)
    return head[:, :128], head[:, 128:256], other[:, :128], other[:, 128:256], last


def unfold_first(part, width):
    tail = width - 256
    last = jnp.where(iota(part.shape[1:], 1) < tail, part[4], 0.0)
    return jnp.concatenate([part[0], part[1], last], axis=1)


def unfold_second(part, width):
    tail = width - 256
    last = jnp.where(iota(part.shape[1:], 1) < tail, pltpu.roll(part[4], 128 - tail, 1), 0.0)
    return jnp.concatenate([part[2], part[3], last], axis=1)


def gather_kernel(blocks, width, spot, swap, swapped, far, dots, out):
    _, second, _ = where_am_i(spot)
    rows, other = swap[...], swapped[...]

    def at(block, i):
        return block[2 * blocks + i : 2 * blocks + i + 1]

    mine, theirs = at(rows, 0), at(other, 0)
    scale = jnp.where(second, mine, jnp.maximum(mine, theirs))
    sent = far[...] * (mine / scale) + jnp.where(
        second, 0.0, other[blocks : 2 * blocks] * (theirs / scale)
    )
    crossing = total(rows[blocks : 2 * blocks] * other[:blocks])
    values = [
        mine[:, :128],
        scale[:, :128],
        (at(rows, 1) + at(other, 1))[:, :128],
        (at(rows, 2) + at(other, 2))[:, :128],
        dots[0:1, 0:1],
        dots[0:1, 1:2] / mine[:, :1],
        at(rows, 2)[:, :128],
        dots[0:1, 2:3],
        jnp.where(second, 0.0, 2.0 * crossing),
        theirs[:, :128],
    ]
    extra = lay_scalars(values, 128, 2 * (width - 256))
    parts = fold(rows[:blocks], sent, width, extra)
    for e in range(out.shape[0]):
        for i, part in enumerate(parts):
            out[e, i] = part


def after_kernel(spot, gathered, out):
    chips = gathered.shape[0]
    chip, _, _ = where_am_i(spot)
    out[...] = gathered[jnp.where(chip == chips - 1, 0, chip + 1)]


def sums_kernel(blocks, width, gathered, out):
    chips = gathered.shape[0]
    tail = width - 256
    table = jnp.concatenate([gathered[e, 4, 0:1, :] for e in range(chips)], axis=0)
    later = jnp.concatenate([table[1:], table[:1]], axis=0)

    def at(i, rows=table):
        return rows[:, 2 * tail + i : 2 * tail + i + 1]

    def chips_total(value):
        return jnp.sum(value, axis=0, keepdims=True)

    norm = chips_total(at(2))
    along = chips_total(at(3))
    alpha = norm / along
    size = alpha * at(0)
    fresh = chips_total(size * (size * at(5) - at(4)) - alpha * at(6))
    diagonal = chips_total(
        size * (size * at(7) + (alpha * at(9)) * at(8) - 2.0 * at(0) * at(5))
    )
    weight = (alpha * at(1)) * (alpha * at(0, later))
    inside = iota((blocks, 128), 1) < tail
    lines = []
    for e in range(chips):
        n = (e + 1) % chips
        ends = jnp.where(inside, pltpu.roll(gathered[e, 4], 128 - tail, 1) * gathered[n, 4], 0.0)
        pair = gathered[e, 2] * gathered[n, 0] + gathered[e, 3] * gathered[n, 1] + ends
        lines.append(jnp.sum(pair, axis=0, keepdims=True))
    edges = total(jnp.concatenate(lines, axis=0) * weight)
    values = [fresh, diagonal + 2.0 * edges, norm, along, alpha, 1.0 / norm, along / norm]
    for i, value in enumerate(values):
        out[i : i + 1, :] = jnp.broadcast_to(value, (1, out.shape[1]))


def prepare_kernel(blocks, width, spot, swap, swapped, near, gathered, next_part, sums,
                   known, scaled, factor, wide):
    chips = gathered.shape[0]
    chip, second, _ = where_am_i(spot)
    tail = width - 256
    before = gathered[jnp.where(chip == 0, chips - 1, chip - 1)]
    ahead = next_part[...]
    alpha = sums[4:5, :]

    def at(part, i):
        return alpha * part[4, 0:1, 2 * tail + i : 2 * tail + i + 1]

    mine = alpha * swap[2 * blocks : 2 * blocks + 1, :]
    theirs = alpha * swapped[2 * blocks : 2 * blocks + 1, :]
    w = swap[:blocks, :] * mine
    scaled[...] = w
    factor[...] = at(ahead, 9)
    spread_rows(wide, w, 0)
    spread_rows(wide, swapped[:blocks, :] * theirs, blocks)
    spread_rows(wide, unfold_first(ahead, width) * at(ahead, 0), 2 * blocks)
    here = near[...] * mine + unfold_second(before, width) * at(before, 1)
    known[...] = here + jnp.where(second, swapped[blocks : 2 * blocks, :] * theirs, 0.0)


def later_kernel(blocks, slots, width,
                 place, live, spot, tiles, known, factor, ready, next_other,
                 product, wide):
    _, second, _ = where_am_i(spot)
    wide[...] = ready[...]

    @pl.when(second)
    def _():
        spread_rows(wide, unfold_first(next_other[...], width) * factor[...], blocks)

    for g in range(blocks):
        columns = upper_columns(tiles, place, live, wide, g, slots, width)
        product[g : g + 1, :] = known[g : g + 1, :] + columns_to_row(columns, width)


def end_kernel(blocks, width, right, z_ref, image, product, scaled, sums, sums_other,
               update, residual):
    norm, along = sums[2:3, :], sums[3:4, :]
    alpha = sums[4:5, :]
    fresh = norm + (sums[0:1, :] + sums_other[0:1, :])
    curved = along + (sums[1:2, :] + sums_other[1:2, :])
    ratio = fresh * sums[5:6, :]
    step = fresh / (curved - ratio * (fresh * sums[6:7, :]))
    z, q = z_ref[...], image[...]
    z_next = z - scaled[...]
    update[...] = (alpha * z + step * (z_next + ratio * z))[:, :width]
    r_next = right[...] - (alpha * q)[:, :width]
    residual[...] = r_next - (step * ((q - product[...]) + ratio * q))[:, :width]


def on_device(right_side, schur_tiles, block_cols, tile_counts, jacobi_inverse):
    count = lax.axis_size(AXIS)
    blocks, slots, width, _ = schur_tiles.shape
    lanes = padded(width)
    chips = count // 2
    vmem = pl.BlockSpec(memory_space=pltpu.VMEM)
    smem = pl.BlockSpec(memory_space=pltpu.SMEM)
    hbm = pl.BlockSpec(memory_space=pltpu.HBM)
    rows = pltpu.VMEM((2 * blocks, lanes), F32)
    half = pltpu.VMEM((blocks, lanes), F32)
    small = pltpu.VMEM((8, lanes), F32)
    more = pltpu.VMEM((4 * blocks, lanes), F32)
    spread = pltpu.VMEM(((BAND + 1) * blocks, 8, lanes), F32)
    index = pltpu.SMEM((blocks, slots), jnp.int32)
    late = pltpu.VMEM((blocks, 8, lanes), F32)

    def call(kernel, sizes, in_specs, out_shape, scratch=(), work=0):
        single = not isinstance(out_shape, list)
        shapes = [out_shape] if single else out_shape
        specs = [
            smem if getattr(shape, "memory_space", None) == pltpu.SMEM else vmem
            for shape in shapes
        ]
        return pl.pallas_call(
            functools.partial(kernel, *sizes),
            in_specs=in_specs,
            out_specs=specs[0] if single else specs,
            out_shape=out_shape,
            scratch_shapes=list(scratch),
            compiler_params=pltpu.CompilerParams(vmem_limit_bytes=VMEM_LIMIT),
            cost_estimate=pl.CostEstimate(
                flops=2 * work * width * width, bytes_accessed=4 * work * width * width, transcendentals=0
            ),
        )

    def swap_cores(value):
        return lax.ppermute(value, AXIS, [(i, i ^ 1) for i in range(count)])

    def swap_chips(odd, value):
        pairs = []
        for i in range(count):
            chip, core = divmod(i, 2)
            step = 1 if (chip % 2 == 1) == odd else -1
            pairs.append((i, 2 * ((chip + step) % chips) + core))
        return lax.ppermute(value, AXIS, pairs)

    sizes = (blocks, slots, width)
    off_chip = [
        pltpu.with_memory_space_constraint(value, pltpu.HBM)
        for value in (block_cols, tile_counts, right_side, jacobi_inverse, schur_tiles)
    ]
    jacobi, tiles, right, place, live, spot, z, near, one_out, odd_out, back_out, even_out = call(
        begin_kernel, sizes + (count,), [hbm] * 5,
        [
            pltpu.VMEM(jacobi_inverse.shape, F32),
            pltpu.VMEM((blocks, slots - 1, width, width), F32),
            pltpu.VMEM(right_side.shape, F32),
            index, index, pltpu.SMEM((4,), jnp.int32),
            half, late, half, half, half, half,
        ],
        [
            pltpu.SMEM(block_cols.shape, jnp.int32),
            pltpu.SMEM(tile_counts.shape, jnp.int32),
            spread,
            pltpu.SemaphoreType.DMA((3,)),
            pltpu.SemaphoreType.DMA((blocks,)),
            pltpu.SemaphoreType.DMA((blocks, slots - 1)),
        ],
        work=blocks * slots,
    )(*off_chip)
    forward_in = lax.ppermute(one_out, AXIS, [(i, (i + 1) % count) for i in range(count)])
    odd_in = swap_chips(True, odd_out)
    back_in = lax.ppermute(back_out, AXIS, [((i + 1) % count, i) for i in range(count)])
    even_in = swap_chips(False, even_out)
    diagonal, near1 = call(
        first_diagonal_kernel, (blocks, width), [hbm, vmem, vmem],
        [pltpu.VMEM((blocks, width, width), F32), half],
        [pltpu.SemaphoreType.DMA((blocks,))],
        work=blocks,
    )(off_chip[4], z, near)
    known, one, two = call(join_kernel, (), [smem] + [vmem] * 5, [half, half, half])(
        spot, near1, forward_in, odd_in, back_in, even_in
    )
    image, swap, far, near2 = call(
        middle_kernel, sizes, [smem] * 2 + [vmem] * 7, [half, more, half, half], [spread, spread],
        work=3 * blocks * slots,
    )(place, live, tiles, jacobi, z, known, one, two, right)
    swapped = swap_cores(swap)
    near3, dots = call(
        second_diagonal_kernel, (blocks, width), [vmem] * 5, [half, pltpu.VMEM((1, 128), F32)], work=blocks
    )(right, diagonal, image, swap, near2)
    sent = call(
        gather_kernel, (blocks, width), [smem] + [vmem] * 4, pltpu.VMEM((chips, 5, blocks, 128), F32)
    )(spot, swap, swapped, far, dots)
    groups = [[2 * c + core for c in range(chips)] for core in range(2)]
    gathered = lax.all_to_all(sent, AXIS, 0, 0, axis_index_groups=groups)
    next_part = call(after_kernel, (), [smem, vmem], pltpu.VMEM((5, blocks, 128), F32))(spot, gathered)
    next_other = swap_cores(next_part)
    sums = call(sums_kernel, (blocks, width), [vmem], small, work=chips)(gathered)
    sums_other = swap_cores(sums)
    known2, scaled, factor, ready = call(
        prepare_kernel, (blocks, width), [smem] + [vmem] * 6,
        [half, half, pltpu.VMEM((1, lanes), F32), spread],
    )(spot, swap, swapped, near3, gathered, next_part, sums)
    product = call(
        later_kernel, sizes, [smem] * 3 + [vmem] * 5, half, [spread], work=100 * blocks * slots,
    )(place, live, spot, tiles, known2, factor, ready, next_other)
    out = jax.ShapeDtypeStruct(right_side.shape, F32)
    return call(end_kernel, (blocks, width), [vmem] * 7, [out, out])(
        right, z, image, product, scaled, sums, sums_other
    )


def solution(mesh):
    placed = (
        P(AXIS, None),
        P(AXIS, None, None, None),
        P(AXIS, None),
        P(AXIS),
        P(AXIS, None, None),
    )
    return jax.shard_map(
        on_device,
        mesh=mesh,
        in_specs=placed,
        out_specs=(P(AXIS, None), P(AXIS, None)),
        check_vma=False,
    )
```

```python
import functools

import jax
import jax.numpy as jnp
from jax import lax
from jax.experimental import pallas as pl
from jax.experimental.pallas import tpu as pltpu
from jax.sharding import PartitionSpec as P

AXIS = "cams"
BAND = 2
F32 = jnp.float32
VMEM_LIMIT = 40 * 2**20
TINY = 1e-30


def padded(width):
    return -(-width // 128) * 128


def iota(shape, dim):
    return lax.broadcasted_iota(jnp.int32, shape, dim)


def total(value):
    return jnp.sum(jnp.sum(value, axis=1, keepdims=True), axis=0, keepdims=True)


def lay_scalars(values, lanes, first):
    lane = iota((1, lanes), 1)
    row = jnp.zeros((1, lanes), F32)
    for i, value in enumerate(values):
        row = jnp.where(lane == first + i, value, row)
    return row


def columns_to_row(columns, width):
    lanes = padded(width)
    skew = iota((8, 128), 1) - iota((8, 128), 0)
    parts = [jnp.zeros((8, 128), F32) for _ in range(lanes // 128)]
    for i, piece in enumerate(columns):
        tile, lane = divmod(8 * i, 128)
        parts[tile] = parts[tile] + jnp.where(skew == lane, piece, 0.0)
    return jnp.sum(jnp.concatenate(parts, axis=1), axis=0, keepdims=True)


def times_row(load, row, width):
    wide = jnp.broadcast_to(row[:, :width], (8, width))
    return [
        jnp.sum(load(i) * wide, axis=1, keepdims=True) for i in range(width // 8)
    ]


def scatter_products(tiles, place, live, group, columns, slots, width, spread):
    sums = [jnp.zeros((8, width), F32) for _ in range(1, slots)]
    for i, piece in enumerate(columns):
        for slot in range(1, slots):
            part = tiles[group, slot - 1, 8 * i : 8 * i + 8, :] * piece
            sums[slot - 1] = sums[slot - 1] + part
    for slot in range(1, slots):
        where = place[group, slot]
        kept = jnp.where(live[group, slot] > 0, sums[slot - 1], 0.0)
        spread[where, :, :width] = spread[where, :, :width] + kept


def upper_columns(tiles, place, live, wide, group, slots, width):
    rows = []
    for slot in range(1, slots):
        row = wide[place[group, slot], :, :width]
        rows.append(jnp.where(live[group, slot] > 0, row, 0.0))
    pieces = []
    for i in range(width // 8):
        part = tiles[group, 0, 8 * i : 8 * i + 8, :] * rows[0]
        for slot in range(2, slots):
            part = part + tiles[group, slot - 1, 8 * i : 8 * i + 8, :] * rows[slot - 1]
        pieces.append(jnp.sum(part, axis=1, keepdims=True))
    return pieces


def where_am_i(spot):
    return spot[0], spot[1] == 1, spot[2] == 1


def begin_kernel(blocks, slots, width, count,
                 cols_hbm, counts_hbm, right_hbm, jacobi_hbm, tiles_hbm,
                 jacobi, tiles, right, place, live, spot, z, near, one_out, odd_out, back_out, even_out,
                 cols, counts, spread, sems, jacobi_sem, tile_sem):
    small = [
        pltpu.make_async_copy(counts_hbm, counts, sems.at[0]),
        pltpu.make_async_copy(cols_hbm, cols, sems.at[1]),
        pltpu.make_async_copy(right_hbm, right, sems.at[2]),
    ]

    def jacobi_copy(g):
        return pltpu.make_async_copy(jacobi_hbm.at[g], jacobi.at[g], jacobi_sem.at[g])

    def tile_copy(g, k):
        return pltpu.make_async_copy(
            tiles_hbm.at[g, k], tiles.at[g, k - 1], tile_sem.at[g, k - 1]
        )

    for copy in small:
        copy.start()
    for g in range(blocks):
        jacobi_copy(g).start()
    small[0].wait()

    @pl.loop(0, blocks)
    def _(g):
        @pl.loop(1, counts[g])
        def _(k):
            tile_copy(g, k).start()

    @pl.loop(0, blocks)
    def _(g):
        @pl.loop(counts[g], slots)
        def _(k):
            tiles[g, k - 1] = jnp.zeros((width, width), F32)

    small[1].wait()
    base = cols[0, 0]
    me = base // blocks
    spot[0] = me // 2
    spot[1] = me % 2
    spot[2] = (me // 2) % 2
    for g in range(blocks):
        for k in range(slots):
            ahead = cols[g, k] - base
            ahead = jnp.where(ahead < 0, ahead + count * blocks, ahead)
            place[g, k] = jnp.clip(ahead, 0, (BAND + 1) * blocks - 1)
            live[g, k] = (k < counts[g]).astype(jnp.int32)
    spread[...] = jnp.zeros_like(spread)
    small[2].wait()

    every = []
    for g in range(blocks):
        jacobi_copy(g).wait()
        columns = times_row(
            lambda i: jacobi[g, 8 * i : 8 * i + 8, :], right[g : g + 1, :], width
        )
        z[g : g + 1, :] = columns_to_row(columns, width)
        every.append(columns)
    for g in range(blocks):
        columns = every[g]

        @pl.loop(1, counts[g])
        def _(k):
            tile_copy(g, k).wait()

        scatter_products(tiles, place, live, g, columns, slots, width, spread)
    near[...] = spread[:blocks]
    sums = jnp.sum(spread[blocks:], axis=1)
    one, two = sums[:blocks], sums[blocks:]
    _, _, odd = where_am_i(spot)
    rows = z[...]
    one_out[...] = one
    back_out[...] = rows
    odd_out[...] = jnp.where(odd, two, rows)
    even_out[...] = jnp.where(odd, rows, two)


def diagonal_product(blocks, width, diagonal, rows, out):
    for g in range(blocks):
        columns = times_row(
            lambda i: diagonal[g, 8 * i : 8 * i + 8, :], rows[g : g + 1, :], width
        )
        out[g : g + 1, :] = columns_to_row(columns, width)


def first_diagonal_kernel(blocks, width, tiles_hbm, z, near, diagonal, near_out, sem):
    copies = [
        pltpu.make_async_copy(tiles_hbm.at[g, 0], diagonal.at[g], sem.at[g])
        for g in range(blocks)
    ]
    for copy in copies:
        copy.start()
    for copy in copies:
        copy.wait()
    diagonal_product(blocks, width, diagonal, z, near_out)
    near_out[...] = near_out[...] + jnp.sum(near[...], axis=1)


def join_kernel(spot, near, forward_in, odd_in, back_in, even_in, known, one, two):
    _, _, odd = where_am_i(spot)
    one[...] = back_in[...]
    two[...] = jnp.where(odd, odd_in[...], even_in[...])
    known[...] = near[...] + forward_in[...] + jnp.where(odd, even_in[...], odd_in[...])


def spread_rows(wide, rows, first):
    for i in range(rows.shape[0]):
        wide[first + i, :, :] = jnp.broadcast_to(rows[i : i + 1], wide.shape[1:])


def middle_kernel(blocks, slots, width,
                  place, live, tiles, jacobi, z, known, one, two, right,
                  image, swap, far, near, wide, spread):
    lanes = padded(width)
    spread_rows(wide, z[...], 0)
    spread_rows(wide, one[...], blocks)
    spread_rows(wide, two[...], 2 * blocks)
    spread[...] = jnp.zeros_like(spread)
    for g in range(blocks):
        columns = upper_columns(tiles, place, live, wide, g, slots, width)
        image[g : g + 1, :] = known[g : g + 1, :] + columns_to_row(columns, width)
    q = image[...]
    size = jnp.max(jnp.max(jnp.abs(q), axis=1, keepdims=True), axis=0, keepdims=True)
    size = jnp.where(size > TINY, size, 1.0)
    scaled = q * (1.0 / size)
    for g in range(blocks):
        columns = times_row(
            lambda i: jacobi[g, 8 * i : 8 * i + 8, :], scaled[g : g + 1, :], width
        )
        swap[g : g + 1, :] = columns_to_row(columns, width)
        scatter_products(tiles, place, live, g, columns, slots, width, spread)
    sums = jnp.sum(spread[...], axis=1)
    far[...] = sums[2 * blocks :]
    near[...] = sums[:blocks]
    swap[blocks : 2 * blocks, :] = sums[blocks : 2 * blocks]
    values = [size, total(right[...] * z[:, :width]), total(z[...] * q)]
    for i, value in enumerate(values):
        swap[2 * blocks + i : 2 * blocks + i + 1, :] = jnp.broadcast_to(value, (1, lanes))


def second_diagonal_kernel(blocks, width, right, diagonal_tiles, image, swap, near, near_out, out):
    w = swap[:blocks, :]
    diagonal_product(blocks, width, diagonal_tiles, swap, near_out)
    diagonal = near_out[...]
    values = [
        total(right[...] * w[:, :width]),
        total(image[...] * w),
        total(w * (diagonal + 2.0 * near[...])),
    ]
    near_out[...] = diagonal + near[...]
    out[...] = lay_scalars(values, 128, 0)


def fold(head, other, width, extra):
    tail = width - 256
    lane = iota((head.shape[0], 128), 1)
    last = jnp.where(lane < tail, head[:, 256:384], pltpu.roll(other[:, 256:384], tail, 1))
    last = jnp.where(lane < 2 * tail, last, extra)
    return head[:, :128], head[:, 128:256], other[:, :128], other[:, 128:256], last


def unfold_first(part, width):
    tail = width - 256
    last = jnp.where(iota(part.shape[1:], 1) < tail, part[4], 0.0)
    return jnp.concatenate([part[0], part[1], last], axis=1)


def unfold_second(part, width):
    tail = width - 256
    last = jnp.where(iota(part.shape[1:], 1) < tail, pltpu.roll(part[4], 128 - tail, 1), 0.0)
    return jnp.concatenate([part[2], part[3], last], axis=1)


def gather_kernel(blocks, width, spot, swap, swapped, far, dots, out):
    _, second, _ = where_am_i(spot)
    rows, other = swap[...], swapped[...]

    def at(block, i):
        return block[2 * blocks + i : 2 * blocks + i + 1]

    mine, theirs = at(rows, 0), at(other, 0)
    scale = jnp.where(second, mine, jnp.maximum(mine, theirs))
    sent = far[...] * (mine / scale) + jnp.where(
        second, 0.0, other[blocks : 2 * blocks] * (theirs / scale)
    )
    crossing = total(rows[blocks : 2 * blocks] * other[:blocks])
    values = [
        mine[:, :128],
        scale[:, :128],
        (at(rows, 1) + at(other, 1))[:, :128],
        (at(rows, 2) + at(other, 2))[:, :128],
        dots[0:1, 0:1],
        dots[0:1, 1:2] / mine[:, :1],
        at(rows, 2)[:, :128],
        dots[0:1, 2:3],
        jnp.where(second, 0.0, 2.0 * crossing),
        theirs[:, :128],
    ]
    extra = lay_scalars(values, 128, 2 * (width - 256))
    parts = fold(rows[:blocks], sent, width, extra)
    for e in range(out.shape[0]):
        for i, part in enumerate(parts):
            out[e, i] = part


def gather_order(chips):
    low, high = chips // 4, chips - chips // 4
    return [*range(high - 1, low - 1, -1), *range(chips - 1, high - 1, -1), *range(low - 1, -1, -1)]


def gather_place(chip, chips):
    low, high = chips // 4, chips - chips // 4
    last = high - low + chips - 1 - chip
    middle = jnp.where(chip >= low, high - 1 - chip, chips - 1 - chip)
    return jnp.where(chip >= high, last, middle)


def after_kernel(spot, gathered, out):
    chips = gathered.shape[0]
    chip, _, _ = where_am_i(spot)
    out[...] = gathered[gather_place(jnp.where(chip == chips - 1, 0, chip + 1), chips)]


def sums_kernel(blocks, width, gathered, out):
    chips = gathered.shape[0]
    tail = width - 256
    order = gather_order(chips)
    places = [order.index(c) for c in range(chips)]
    table = jnp.concatenate([gathered[e, 4, 0:1, :] for e in places], axis=0)
    later = jnp.concatenate([table[1:], table[:1]], axis=0)

    def at(i, rows=table):
        return rows[:, 2 * tail + i : 2 * tail + i + 1]

    def chips_total(value):
        return jnp.sum(value, axis=0, keepdims=True)

    norm = chips_total(at(2))
    along = chips_total(at(3))
    alpha = norm / along
    size = alpha * at(0)
    fresh = chips_total(size * (size * at(5) - at(4)) - alpha * at(6))
    diagonal = chips_total(
        size * (size * at(7) + (alpha * at(9)) * at(8) - 2.0 * at(0) * at(5))
    )
    weight = (alpha * at(1)) * (alpha * at(0, later))
    inside = iota((blocks, 128), 1) < tail
    lines = []
    for e in range(chips):
        n = (e + 1) % chips
        here, there = gathered[places[e]], gathered[places[n]]
        ends = jnp.where(inside, pltpu.roll(here[4], 128 - tail, 1) * there[4], 0.0)
        pair = here[2] * there[0] + here[3] * there[1] + ends
        lines.append(jnp.sum(pair, axis=0, keepdims=True))
    edges = total(jnp.concatenate(lines, axis=0) * weight)
    values = [fresh, diagonal + 2.0 * edges, norm, along, alpha, 1.0 / norm, along / norm]
    for i, value in enumerate(values):
        out[i : i + 1, :] = jnp.broadcast_to(value, (1, out.shape[1]))


def prepare_kernel(blocks, width, spot, swap, swapped, near, gathered, next_part, sums,
                   known, scaled, factor, wide):
    chips = gathered.shape[0]
    chip, second, _ = where_am_i(spot)
    tail = width - 256
    before = gathered[gather_place(jnp.where(chip == 0, chips - 1, chip - 1), chips)]
    ahead = next_part[...]
    alpha = sums[4:5, :]

    def at(part, i):
        return alpha * part[4, 0:1, 2 * tail + i : 2 * tail + i + 1]

    mine = alpha * swap[2 * blocks : 2 * blocks + 1, :]
    theirs = alpha * swapped[2 * blocks : 2 * blocks + 1, :]
    w = swap[:blocks, :] * mine
    scaled[...] = w
    factor[...] = at(ahead, 9)
    spread_rows(wide, w, 0)
    spread_rows(wide, swapped[:blocks, :] * theirs, blocks)
    spread_rows(wide, unfold_first(ahead, width) * at(ahead, 0), 2 * blocks)
    here = near[...] * mine + unfold_second(before, width) * at(before, 1)
    known[...] = here + jnp.where(second, swapped[blocks : 2 * blocks, :] * theirs, 0.0)


def later_kernel(blocks, slots, width,
                 place, live, spot, tiles, known, factor, ready, next_other,
                 product, wide):
    _, second, _ = where_am_i(spot)
    wide[...] = ready[...]

    @pl.when(second)
    def _():
        spread_rows(wide, unfold_first(next_other[...], width) * factor[...], blocks)

    for g in range(blocks):
        columns = upper_columns(tiles, place, live, wide, g, slots, width)
        product[g : g + 1, :] = known[g : g + 1, :] + columns_to_row(columns, width)


def end_kernel(blocks, width, right, z_ref, image, product, scaled, sums, sums_other,
               update, residual):
    norm, along = sums[2:3, :], sums[3:4, :]
    alpha = sums[4:5, :]
    fresh = norm + (sums[0:1, :] + sums_other[0:1, :])
    curved = along + (sums[1:2, :] + sums_other[1:2, :])
    ratio = fresh * sums[5:6, :]
    step = fresh / (curved - ratio * (fresh * sums[6:7, :]))
    z, q = z_ref[...], image[...]
    z_next = z - scaled[...]
    update[...] = (alpha * z + step * (z_next + ratio * z))[:, :width]
    r_next = right[...] - (alpha * q)[:, :width]
    residual[...] = r_next - (step * ((q - product[...]) + ratio * q))[:, :width]


def on_device(right_side, schur_tiles, block_cols, tile_counts, jacobi_inverse):
    count = lax.axis_size(AXIS)
    blocks, slots, width, _ = schur_tiles.shape
    lanes = padded(width)
    chips = count // 2
    vmem = pl.BlockSpec(memory_space=pltpu.VMEM)
    smem = pl.BlockSpec(memory_space=pltpu.SMEM)
    hbm = pl.BlockSpec(memory_space=pltpu.HBM)
    rows = pltpu.VMEM((2 * blocks, lanes), F32)
    half = pltpu.VMEM((blocks, lanes), F32)
    small = pltpu.VMEM((8, lanes), F32)
    more = pltpu.VMEM((4 * blocks, lanes), F32)
    spread = pltpu.VMEM(((BAND + 1) * blocks, 8, lanes), F32)
    index = pltpu.SMEM((blocks, slots), jnp.int32)
    late = pltpu.VMEM((blocks, 8, lanes), F32)

    def call(kernel, sizes, in_specs, out_shape, scratch=(), work=0):
        single = not isinstance(out_shape, list)
        shapes = [out_shape] if single else out_shape
        specs = [
            smem if getattr(shape, "memory_space", None) == pltpu.SMEM else vmem
            for shape in shapes
        ]
        return pl.pallas_call(
            functools.partial(kernel, *sizes),
            in_specs=in_specs,
            out_specs=specs[0] if single else specs,
            out_shape=out_shape,
            scratch_shapes=list(scratch),
            compiler_params=pltpu.CompilerParams(vmem_limit_bytes=VMEM_LIMIT),
            cost_estimate=pl.CostEstimate(
                flops=2 * work * width * width, bytes_accessed=4 * work * width * width, transcendentals=0
            ),
        )

    def swap_cores(value):
        return lax.ppermute(value, AXIS, [(i, i ^ 1) for i in range(count)])

    def swap_chips(odd, value):
        pairs = []
        for i in range(count):
            chip, core = divmod(i, 2)
            step = 1 if (chip % 2 == 1) == odd else -1
            pairs.append((i, 2 * ((chip + step) % chips) + core))
        return lax.ppermute(value, AXIS, pairs)

    sizes = (blocks, slots, width)
    off_chip = [
        pltpu.with_memory_space_constraint(value, pltpu.HBM)
        for value in (block_cols, tile_counts, right_side, jacobi_inverse, schur_tiles)
    ]
    jacobi, tiles, right, place, live, spot, z, near, one_out, odd_out, back_out, even_out = call(
        begin_kernel, sizes + (count,), [hbm] * 5,
        [
            pltpu.VMEM(jacobi_inverse.shape, F32),
            pltpu.VMEM((blocks, slots - 1, width, width), F32),
            pltpu.VMEM(right_side.shape, F32),
            index, index, pltpu.SMEM((4,), jnp.int32),
            half, late, half, half, half, half,
        ],
        [
            pltpu.SMEM(block_cols.shape, jnp.int32),
            pltpu.SMEM(tile_counts.shape, jnp.int32),
            spread,
            pltpu.SemaphoreType.DMA((3,)),
            pltpu.SemaphoreType.DMA((blocks,)),
            pltpu.SemaphoreType.DMA((blocks, slots - 1)),
        ],
        work=blocks * slots,
    )(*off_chip)
    forward_in = lax.ppermute(one_out, AXIS, [(i, (i + 1) % count) for i in range(count)])
    odd_in = swap_chips(True, odd_out)
    back_in = lax.ppermute(back_out, AXIS, [((i + 1) % count, i) for i in range(count)])
    even_in = swap_chips(False, even_out)
    diagonal, near1 = call(
        first_diagonal_kernel, (blocks, width), [hbm, vmem, vmem],
        [pltpu.VMEM((blocks, width, width), F32), half],
        [pltpu.SemaphoreType.DMA((blocks,))],
        work=blocks,
    )(off_chip[4], z, near)
    known, one, two = call(join_kernel, (), [smem] + [vmem] * 5, [half, half, half])(
        spot, near1, forward_in, odd_in, back_in, even_in
    )
    image, swap, far, near2 = call(
        middle_kernel, sizes, [smem] * 2 + [vmem] * 7, [half, more, half, half], [spread, spread],
        work=3 * blocks * slots,
    )(place, live, tiles, jacobi, z, known, one, two, right)
    swapped = swap_cores(swap)
    near3, dots = call(
        second_diagonal_kernel, (blocks, width), [vmem] * 5, [half, pltpu.VMEM((1, 128), F32)], work=blocks
    )(right, diagonal, image, swap, near2)
    sent = call(
        gather_kernel, (blocks, width), [smem] + [vmem] * 4, pltpu.VMEM((chips, 5, blocks, 128), F32)
    )(spot, swap, swapped, far, dots)
    groups = [[2 * c + core for c in gather_order(chips)] for core in range(2)]
    gathered = lax.all_to_all(sent, AXIS, 0, 0, axis_index_groups=groups)
    next_part = call(after_kernel, (), [smem, vmem], pltpu.VMEM((5, blocks, 128), F32))(spot, gathered)
    next_other = swap_cores(next_part)
    sums = call(sums_kernel, (blocks, width), [vmem], small, work=chips)(gathered)
    sums_other = swap_cores(sums)
    known2, scaled, factor, ready = call(
        prepare_kernel, (blocks, width), [smem] + [vmem] * 6,
        [half, half, pltpu.VMEM((1, lanes), F32), spread],
    )(spot, swap, swapped, near3, gathered, next_part, sums)
    product = call(
        later_kernel, sizes, [smem] * 3 + [vmem] * 5, half, [spread], work=100 * blocks * slots,
    )(place, live, spot, tiles, known2, factor, ready, next_other)
    out = jax.ShapeDtypeStruct(right_side.shape, F32)
    return call(end_kernel, (blocks, width), [vmem] * 7, [out, out])(
        right, z, image, product, scaled, sums, sums_other
    )


def solution(mesh):
    placed = (
        P(AXIS, None),
        P(AXIS, None, None, None),
        P(AXIS, None),
        P(AXIS),
        P(AXIS, None, None),
    )
    return jax.shard_map(
        on_device,
        mesh=mesh,
        in_specs=placed,
        out_specs=(P(AXIS, None), P(AXIS, None)),
        check_vma=False,
    )
```

```python
import functools

import jax
import jax.numpy as jnp
from jax import lax
from jax.experimental import pallas as pl
from jax.experimental.pallas import tpu as pltpu
from jax.sharding import PartitionSpec as P

AXIS = "cams"
BAND = 2
F32 = jnp.float32
VMEM_LIMIT = 40 * 2**20
TINY = 1e-30


def padded(width):
    return -(-width // 128) * 128


def iota(shape, dim):
    return lax.broadcasted_iota(jnp.int32, shape, dim)


def total(value):
    return jnp.sum(jnp.sum(value, axis=1, keepdims=True), axis=0, keepdims=True)


def lay_scalars(values, lanes, first):
    lane = iota((1, lanes), 1)
    row = jnp.zeros((1, lanes), F32)
    for i, value in enumerate(values):
        row = jnp.where(lane == first + i, value, row)
    return row


def columns_to_row(columns, width):
    lanes = padded(width)
    skew = iota((8, 128), 1) - iota((8, 128), 0)
    parts = [jnp.zeros((8, 128), F32) for _ in range(lanes // 128)]
    for i, piece in enumerate(columns):
        tile, lane = divmod(8 * i, 128)
        parts[tile] = parts[tile] + jnp.where(skew == lane, piece, 0.0)
    return jnp.sum(jnp.concatenate(parts, axis=1), axis=0, keepdims=True)


def times_row(load, row, width):
    wide = jnp.broadcast_to(row[:, :width], (8, width))
    return [
        jnp.sum(load(i) * wide, axis=1, keepdims=True) for i in range(width // 8)
    ]


def scatter_products(tiles, place, live, group, columns, slots, width, spread):
    sums = [jnp.zeros((8, width), F32) for _ in range(1, slots)]
    for i, piece in enumerate(columns):
        for slot in range(1, slots):
            part = tiles[group, slot - 1, 8 * i : 8 * i + 8, :] * piece
            sums[slot - 1] = sums[slot - 1] + part
    for slot in range(1, slots):
        where = place[group, slot]
        kept = jnp.where(live[group, slot] > 0, sums[slot - 1], 0.0)
        spread[where, :, :width] = spread[where, :, :width] + kept


def upper_columns(tiles, place, live, wide, group, slots, width):
    rows = []
    for slot in range(1, slots):
        row = wide[place[group, slot], :, :width]
        rows.append(jnp.where(live[group, slot] > 0, row, 0.0))
    pieces = []
    for i in range(width // 8):
        part = tiles[group, 0, 8 * i : 8 * i + 8, :] * rows[0]
        for slot in range(2, slots):
            part = part + tiles[group, slot - 1, 8 * i : 8 * i + 8, :] * rows[slot - 1]
        pieces.append(jnp.sum(part, axis=1, keepdims=True))
    return pieces


def where_am_i(spot):
    return spot[0], spot[1] == 1, spot[2] == 1


def begin_kernel(blocks, slots, width, count,
                 cols_hbm, counts_hbm, right_hbm, jacobi_hbm, tiles_hbm,
                 jacobi, tiles, right, place, live, spot, z, near, one_out, odd_out, back_out, even_out,
                 cols, counts, spread, sems, jacobi_sem, tile_sem):
    small = [
        pltpu.make_async_copy(counts_hbm, counts, sems.at[0]),
        pltpu.make_async_copy(cols_hbm, cols, sems.at[1]),
        pltpu.make_async_copy(right_hbm, right, sems.at[2]),
    ]

    def jacobi_copy(g):
        return pltpu.make_async_copy(jacobi_hbm.at[g], jacobi.at[g], jacobi_sem.at[g])

    def tile_copy(g, k):
        return pltpu.make_async_copy(
            tiles_hbm.at[g, k], tiles.at[g, k - 1], tile_sem.at[g, k - 1]
        )

    for copy in small:
        copy.start()
    for g in range(blocks):
        jacobi_copy(g).start()
    small[0].wait()

    @pl.loop(0, blocks)
    def _(g):
        @pl.loop(1, counts[g])
        def _(k):
            tile_copy(g, k).start(priority=1)

    @pl.loop(0, blocks)
    def _(g):
        @pl.loop(counts[g], slots)
        def _(k):
            tiles[g, k - 1] = jnp.zeros((width, width), F32)

    small[1].wait()
    base = cols[0, 0]
    me = base // blocks
    spot[0] = me // 2
    spot[1] = me % 2
    spot[2] = (me // 2) % 2
    for g in range(blocks):
        for k in range(slots):
            ahead = cols[g, k] - base
            ahead = jnp.where(ahead < 0, ahead + count * blocks, ahead)
            place[g, k] = jnp.clip(ahead, 0, (BAND + 1) * blocks - 1)
            live[g, k] = (k < counts[g]).astype(jnp.int32)
    spread[...] = jnp.zeros_like(spread)
    small[2].wait()

    every = []
    for g in range(blocks):
        jacobi_copy(g).wait()
        columns = times_row(
            lambda i: jacobi[g, 8 * i : 8 * i + 8, :], right[g : g + 1, :], width
        )
        z[g : g + 1, :] = columns_to_row(columns, width)
        every.append(columns)
    for g in range(blocks):
        columns = every[g]

        @pl.loop(1, counts[g])
        def _(k):
            tile_copy(g, k).wait()

        scatter_products(tiles, place, live, g, columns, slots, width, spread)
    near[...] = spread[:blocks]
    sums = jnp.sum(spread[blocks:], axis=1)
    one, two = sums[:blocks], sums[blocks:]
    _, _, odd = where_am_i(spot)
    rows = z[...]
    one_out[...] = one
    back_out[...] = rows
    odd_out[...] = jnp.where(odd, two, rows)
    even_out[...] = jnp.where(odd, rows, two)


def diagonal_product(blocks, width, diagonal, rows, out):
    for g in range(blocks):
        columns = times_row(
            lambda i: diagonal[g, 8 * i : 8 * i + 8, :], rows[g : g + 1, :], width
        )
        out[g : g + 1, :] = columns_to_row(columns, width)


def first_diagonal_kernel(blocks, width, tiles_hbm, z, near, diagonal, near_out, sem):
    copies = [
        pltpu.make_async_copy(tiles_hbm.at[g, 0], diagonal.at[g], sem.at[g])
        for g in range(blocks)
    ]
    for copy in copies:
        copy.start()
    for copy in copies:
        copy.wait()
    diagonal_product(blocks, width, diagonal, z, near_out)
    near_out[...] = near_out[...] + jnp.sum(near[...], axis=1)


def join_kernel(spot, near, forward_in, odd_in, back_in, even_in, known, one, two):
    _, _, odd = where_am_i(spot)
    one[...] = back_in[...]
    two[...] = jnp.where(odd, odd_in[...], even_in[...])
    known[...] = near[...] + forward_in[...] + jnp.where(odd, even_in[...], odd_in[...])


def spread_rows(wide, rows, first):
    for i in range(rows.shape[0]):
        wide[first + i, :, :] = jnp.broadcast_to(rows[i : i + 1], wide.shape[1:])


def middle_kernel(blocks, slots, width,
                  place, live, tiles, jacobi, z, known, one, two, right,
                  image, swap, far, near, wide, spread):
    lanes = padded(width)
    spread_rows(wide, z[...], 0)
    spread_rows(wide, one[...], blocks)
    spread_rows(wide, two[...], 2 * blocks)
    spread[...] = jnp.zeros_like(spread)
    for g in range(blocks):
        columns = upper_columns(tiles, place, live, wide, g, slots, width)
        image[g : g + 1, :] = known[g : g + 1, :] + columns_to_row(columns, width)
    q = image[...]
    size = jnp.max(jnp.max(jnp.abs(q), axis=1, keepdims=True), axis=0, keepdims=True)
    size = jnp.where(size > TINY, size, 1.0)
    scaled = q * (1.0 / size)
    for g in range(blocks):
        columns = times_row(
            lambda i: jacobi[g, 8 * i : 8 * i + 8, :], scaled[g : g + 1, :], width
        )
        swap[g : g + 1, :] = columns_to_row(columns, width)
        scatter_products(tiles, place, live, g, columns, slots, width, spread)
    sums = jnp.sum(spread[...], axis=1)
    far[...] = sums[2 * blocks :]
    near[...] = sums[:blocks]
    swap[blocks : 2 * blocks, :] = sums[blocks : 2 * blocks]
    values = [size, total(right[...] * z[:, :width]), total(z[...] * q)]
    for i, value in enumerate(values):
        swap[2 * blocks + i : 2 * blocks + i + 1, :] = jnp.broadcast_to(value, (1, lanes))


def second_diagonal_kernel(blocks, width, right, diagonal_tiles, image, swap, near, near_out, out):
    w = swap[:blocks, :]
    diagonal_product(blocks, width, diagonal_tiles, swap, near_out)
    diagonal = near_out[...]
    values = [
        total(right[...] * w[:, :width]),
        total(image[...] * w),
        total(w * (diagonal + 2.0 * near[...])),
    ]
    near_out[...] = diagonal + near[...]
    out[...] = lay_scalars(values, 128, 0)


def fold(head, other, width, extra):
    tail = width - 256
    lane = iota((head.shape[0], 128), 1)
    last = jnp.where(lane < tail, head[:, 256:384], pltpu.roll(other[:, 256:384], tail, 1))
    last = jnp.where(lane < 2 * tail, last, extra)
    return head[:, :128], head[:, 128:256], other[:, :128], other[:, 128:256], last


def unfold_first(part, width):
    tail = width - 256
    last = jnp.where(iota(part.shape[1:], 1) < tail, part[4], 0.0)
    return jnp.concatenate([part[0], part[1], last], axis=1)


def unfold_second(part, width):
    tail = width - 256
    last = jnp.where(iota(part.shape[1:], 1) < tail, pltpu.roll(part[4], 128 - tail, 1), 0.0)
    return jnp.concatenate([part[2], part[3], last], axis=1)


def gather_kernel(blocks, width, spot, swap, swapped, far, dots, out):
    _, second, _ = where_am_i(spot)
    rows, other = swap[...], swapped[...]

    def at(block, i):
        return block[2 * blocks + i : 2 * blocks + i + 1]

    mine, theirs = at(rows, 0), at(other, 0)
    scale = jnp.where(second, mine, jnp.maximum(mine, theirs))
    sent = far[...] * (mine / scale) + jnp.where(
        second, 0.0, other[blocks : 2 * blocks] * (theirs / scale)
    )
    crossing = total(rows[blocks : 2 * blocks] * other[:blocks])
    values = [
        mine[:, :128],
        scale[:, :128],
        (at(rows, 1) + at(other, 1))[:, :128],
        (at(rows, 2) + at(other, 2))[:, :128],
        dots[0:1, 0:1],
        dots[0:1, 1:2] / mine[:, :1],
        at(rows, 2)[:, :128],
        dots[0:1, 2:3],
        jnp.where(second, 0.0, 2.0 * crossing),
        theirs[:, :128],
    ]
    extra = lay_scalars(values, 128, 2 * (width - 256))
    parts = fold(rows[:blocks], sent, width, extra)
    for e in range(out.shape[0]):
        for i, part in enumerate(parts):
            out[e, i] = part


def gather_order(chips):
    low, high = chips // 4, chips - chips // 4
    return [*range(high - 1, low - 1, -1), *range(chips - 1, high - 1, -1), *range(low - 1, -1, -1)]


def gather_place(chip, chips):
    low, high = chips // 4, chips - chips // 4
    last = high - low + chips - 1 - chip
    middle = jnp.where(chip >= low, high - 1 - chip, chips - 1 - chip)
    return jnp.where(chip >= high, last, middle)


def after_kernel(spot, gathered, out):
    chips = gathered.shape[0]
    chip, _, _ = where_am_i(spot)
    out[...] = gathered[gather_place(jnp.where(chip == chips - 1, 0, chip + 1), chips)]


def sums_kernel(blocks, width, gathered, out):
    chips = gathered.shape[0]
    tail = width - 256
    order = gather_order(chips)
    places = [order.index(c) for c in range(chips)]
    table = jnp.concatenate([gathered[e, 4, 0:1, :] for e in places], axis=0)
    later = jnp.concatenate([table[1:], table[:1]], axis=0)

    def at(i, rows=table):
        return rows[:, 2 * tail + i : 2 * tail + i + 1]

    def chips_total(value):
        return jnp.sum(value, axis=0, keepdims=True)

    norm = chips_total(at(2))
    along = chips_total(at(3))
    alpha = norm / along
    size = alpha * at(0)
    fresh = chips_total(size * (size * at(5) - at(4)) - alpha * at(6))
    diagonal = chips_total(
        size * (size * at(7) + (alpha * at(9)) * at(8) - 2.0 * at(0) * at(5))
    )
    weight = (alpha * at(1)) * (alpha * at(0, later))
    inside = iota((blocks, 128), 1) < tail
    lines = []
    for e in range(chips):
        n = (e + 1) % chips
        here, there = gathered[places[e]], gathered[places[n]]
        ends = jnp.where(inside, pltpu.roll(here[4], 128 - tail, 1) * there[4], 0.0)
        pair = here[2] * there[0] + here[3] * there[1] + ends
        lines.append(jnp.sum(pair, axis=0, keepdims=True))
    edges = total(jnp.concatenate(lines, axis=0) * weight)
    values = [fresh, diagonal + 2.0 * edges, norm, along, alpha, 1.0 / norm, along / norm]
    for i, value in enumerate(values):
        out[i : i + 1, :] = jnp.broadcast_to(value, (1, out.shape[1]))


def prepare_kernel(blocks, width, spot, swap, swapped, near, gathered, next_part, sums,
                   known, scaled, factor, wide):
    chips = gathered.shape[0]
    chip, second, _ = where_am_i(spot)
    tail = width - 256
    before = gathered[gather_place(jnp.where(chip == 0, chips - 1, chip - 1), chips)]
    ahead = next_part[...]
    alpha = sums[4:5, :]

    def at(part, i):
        return alpha * part[4, 0:1, 2 * tail + i : 2 * tail + i + 1]

    mine = alpha * swap[2 * blocks : 2 * blocks + 1, :]
    theirs = alpha * swapped[2 * blocks : 2 * blocks + 1, :]
    w = swap[:blocks, :] * mine
    scaled[...] = w
    factor[...] = at(ahead, 9)
    spread_rows(wide, w, 0)
    spread_rows(wide, swapped[:blocks, :] * theirs, blocks)
    spread_rows(wide, unfold_first(ahead, width) * at(ahead, 0), 2 * blocks)
    here = near[...] * mine + unfold_second(before, width) * at(before, 1)
    known[...] = here + jnp.where(second, swapped[blocks : 2 * blocks, :] * theirs, 0.0)


def later_kernel(blocks, slots, width,
                 place, live, spot, tiles, known, factor, ready, next_other,
                 product, wide):
    _, second, _ = where_am_i(spot)
    wide[...] = ready[...]

    @pl.when(second)
    def _():
        spread_rows(wide, unfold_first(next_other[...], width) * factor[...], blocks)

    for g in range(blocks):
        columns = upper_columns(tiles, place, live, wide, g, slots, width)
        product[g : g + 1, :] = known[g : g + 1, :] + columns_to_row(columns, width)


def end_kernel(blocks, width, right, z_ref, image, product, scaled, sums, sums_other,
               update, residual):
    norm, along = sums[2:3, :], sums[3:4, :]
    alpha = sums[4:5, :]
    fresh = norm + (sums[0:1, :] + sums_other[0:1, :])
    curved = along + (sums[1:2, :] + sums_other[1:2, :])
    ratio = fresh * sums[5:6, :]
    step = fresh / (curved - ratio * (fresh * sums[6:7, :]))
    z, q = z_ref[...], image[...]
    z_next = z - scaled[...]
    update[...] = (alpha * z + step * (z_next + ratio * z))[:, :width]
    r_next = right[...] - (alpha * q)[:, :width]
    residual[...] = r_next - (step * ((q - product[...]) + ratio * q))[:, :width]


def on_device(right_side, schur_tiles, block_cols, tile_counts, jacobi_inverse):
    count = lax.axis_size(AXIS)
    blocks, slots, width, _ = schur_tiles.shape
    lanes = padded(width)
    chips = count // 2
    vmem = pl.BlockSpec(memory_space=pltpu.VMEM)
    smem = pl.BlockSpec(memory_space=pltpu.SMEM)
    hbm = pl.BlockSpec(memory_space=pltpu.HBM)
    rows = pltpu.VMEM((2 * blocks, lanes), F32)
    half = pltpu.VMEM((blocks, lanes), F32)
    small = pltpu.VMEM((8, lanes), F32)
    more = pltpu.VMEM((4 * blocks, lanes), F32)
    spread = pltpu.VMEM(((BAND + 1) * blocks, 8, lanes), F32)
    index = pltpu.SMEM((blocks, slots), jnp.int32)
    late = pltpu.VMEM((blocks, 8, lanes), F32)

    def call(kernel, sizes, in_specs, out_shape, scratch=(), work=0):
        single = not isinstance(out_shape, list)
        shapes = [out_shape] if single else out_shape
        specs = [
            smem if getattr(shape, "memory_space", None) == pltpu.SMEM else vmem
            for shape in shapes
        ]
        return pl.pallas_call(
            functools.partial(kernel, *sizes),
            in_specs=in_specs,
            out_specs=specs[0] if single else specs,
            out_shape=out_shape,
            scratch_shapes=list(scratch),
            compiler_params=pltpu.CompilerParams(vmem_limit_bytes=VMEM_LIMIT),
            cost_estimate=pl.CostEstimate(
                flops=2 * work * width * width, bytes_accessed=4 * work * width * width, transcendentals=0
            ),
        )

    def swap_cores(value):
        return lax.ppermute(value, AXIS, [(i, i ^ 1) for i in range(count)])

    def swap_chips(odd, value):
        pairs = []
        for i in range(count):
            chip, core = divmod(i, 2)
            step = 1 if (chip % 2 == 1) == odd else -1
            pairs.append((i, 2 * ((chip + step) % chips) + core))
        return lax.ppermute(value, AXIS, pairs)

    sizes = (blocks, slots, width)
    off_chip = [
        pltpu.with_memory_space_constraint(value, pltpu.HBM)
        for value in (block_cols, tile_counts, right_side, jacobi_inverse, schur_tiles)
    ]
    jacobi, tiles, right, place, live, spot, z, near, one_out, odd_out, back_out, even_out = call(
        begin_kernel, sizes + (count,), [hbm] * 5,
        [
            pltpu.VMEM(jacobi_inverse.shape, F32),
            pltpu.VMEM((blocks, slots - 1, width, width), F32),
            pltpu.VMEM(right_side.shape, F32),
            index, index, pltpu.SMEM((4,), jnp.int32),
            half, late, half, half, half, half,
        ],
        [
            pltpu.SMEM(block_cols.shape, jnp.int32),
            pltpu.SMEM(tile_counts.shape, jnp.int32),
            spread,
            pltpu.SemaphoreType.DMA((3,)),
            pltpu.SemaphoreType.DMA((blocks,)),
            pltpu.SemaphoreType.DMA((blocks, slots - 1)),
        ],
        work=blocks * slots,
    )(*off_chip)
    forward_in = lax.ppermute(one_out, AXIS, [(i, (i + 1) % count) for i in range(count)])
    odd_in = swap_chips(True, odd_out)
    back_in = lax.ppermute(back_out, AXIS, [((i + 1) % count, i) for i in range(count)])
    even_in = swap_chips(False, even_out)
    diagonal, near1 = call(
        first_diagonal_kernel, (blocks, width), [hbm, vmem, vmem],
        [pltpu.VMEM((blocks, width, width), F32), half],
        [pltpu.SemaphoreType.DMA((blocks,))],
        work=blocks,
    )(off_chip[4], z, near)
    known, one, two = call(join_kernel, (), [smem] + [vmem] * 5, [half, half, half])(
        spot, near1, forward_in, odd_in, back_in, even_in
    )
    image, swap, far, near2 = call(
        middle_kernel, sizes, [smem] * 2 + [vmem] * 7, [half, more, half, half], [spread, spread],
        work=3 * blocks * slots,
    )(place, live, tiles, jacobi, z, known, one, two, right)
    swapped = swap_cores(swap)
    near3, dots = call(
        second_diagonal_kernel, (blocks, width), [vmem] * 5, [half, pltpu.VMEM((1, 128), F32)], work=blocks
    )(right, diagonal, image, swap, near2)
    sent = call(
        gather_kernel, (blocks, width), [smem] + [vmem] * 4, pltpu.VMEM((chips, 5, blocks, 128), F32)
    )(spot, swap, swapped, far, dots)
    groups = [[2 * c + core for c in gather_order(chips)] for core in range(2)]
    gathered = lax.all_to_all(sent, AXIS, 0, 0, axis_index_groups=groups)
    next_part = call(after_kernel, (), [smem, vmem], pltpu.VMEM((5, blocks, 128), F32))(spot, gathered)
    next_other = swap_cores(next_part)
    sums = call(sums_kernel, (blocks, width), [vmem], small, work=chips)(gathered)
    sums_other = swap_cores(sums)
    known2, scaled, factor, ready = call(
        prepare_kernel, (blocks, width), [smem] + [vmem] * 6,
        [half, half, pltpu.VMEM((1, lanes), F32), spread],
    )(spot, swap, swapped, near3, gathered, next_part, sums)
    product = call(
        later_kernel, sizes, [smem] * 3 + [vmem] * 5, half, [spread], work=100 * blocks * slots,
    )(place, live, spot, tiles, known2, factor, ready, next_other)
    out = jax.ShapeDtypeStruct(right_side.shape, F32)
    return call(end_kernel, (blocks, width), [vmem] * 7, [out, out])(
        right, z, image, product, scaled, sums, sums_other
    )


def solution(mesh):
    placed = (
        P(AXIS, None),
        P(AXIS, None, None, None),
        P(AXIS, None),
        P(AXIS),
        P(AXIS, None, None),
    )
    return jax.shard_map(
        on_device,
        mesh=mesh,
        in_specs=placed,
        out_specs=(P(AXIS, None), P(AXIS, None)),
        check_vma=False,
    )
```

```python
import functools

import jax
import jax.numpy as jnp
from jax import lax
from jax.experimental import pallas as pl
from jax.experimental.pallas import tpu as pltpu
from jax.sharding import PartitionSpec as P

AXIS = "cams"
BAND = 2
F32 = jnp.float32
VMEM_LIMIT = 40 * 2**20
TINY = 1e-30


def padded(width):
    return -(-width // 128) * 128


def iota(shape, dim):
    return lax.broadcasted_iota(jnp.int32, shape, dim)


def total(value):
    return jnp.sum(jnp.sum(value, axis=1, keepdims=True), axis=0, keepdims=True)


def lay_scalars(values, lanes, first):
    lane = iota((1, lanes), 1)
    row = jnp.zeros((1, lanes), F32)
    for i, value in enumerate(values):
        row = jnp.where(lane == first + i, value, row)
    return row


def columns_to_row(columns, width):
    lanes = padded(width)
    skew = iota((8, 128), 1) - iota((8, 128), 0)
    parts = [jnp.zeros((8, 128), F32) for _ in range(lanes // 128)]
    for i, piece in enumerate(columns):
        tile, lane = divmod(8 * i, 128)
        parts[tile] = parts[tile] + jnp.where(skew == lane, piece, 0.0)
    return jnp.sum(jnp.concatenate(parts, axis=1), axis=0, keepdims=True)


def times_row(load, row, width):
    wide = jnp.broadcast_to(row[:, :width], (8, width))
    return [
        jnp.sum(load(i) * wide, axis=1, keepdims=True) for i in range(width // 8)
    ]


def scatter_products(tiles, place, live, group, columns, slots, width, spread):
    sums = [jnp.zeros((8, width), F32) for _ in range(1, slots)]
    for i, piece in enumerate(columns):
        for slot in range(1, slots):
            part = tiles[group, slot - 1, 8 * i : 8 * i + 8, :] * piece
            sums[slot - 1] = sums[slot - 1] + part
    for slot in range(1, slots):
        where = place[group, slot]
        kept = jnp.where(live[group, slot] > 0, sums[slot - 1], 0.0)
        spread[where, :, :width] = spread[where, :, :width] + kept


def upper_columns(tiles, place, live, wide, group, slots, width):
    rows = []
    for slot in range(1, slots):
        row = wide[place[group, slot], :, :width]
        rows.append(jnp.where(live[group, slot] > 0, row, 0.0))
    pieces = []
    for i in range(width // 8):
        part = tiles[group, 0, 8 * i : 8 * i + 8, :] * rows[0]
        for slot in range(2, slots):
            part = part + tiles[group, slot - 1, 8 * i : 8 * i + 8, :] * rows[slot - 1]
        pieces.append(jnp.sum(part, axis=1, keepdims=True))
    return pieces


def where_am_i(spot):
    return spot[0], spot[1] == 1, spot[2] == 1


def begin_kernel(blocks, slots, width, count,
                 cols_hbm, counts_hbm, right_hbm, jacobi_hbm, tiles_hbm,
                 jacobi, tiles, right, place, live, spot, z, near, one_out, odd_out, back_out, even_out,
                 cols, counts, spread, sems, jacobi_sem, tile_sem):
    small = [
        pltpu.make_async_copy(counts_hbm, counts, sems.at[0]),
        pltpu.make_async_copy(cols_hbm, cols, sems.at[1]),
        pltpu.make_async_copy(right_hbm, right, sems.at[2]),
    ]

    def jacobi_copy(g):
        return pltpu.make_async_copy(jacobi_hbm.at[g], jacobi.at[g], jacobi_sem.at[g])

    def tile_copy(g, k):
        return pltpu.make_async_copy(
            tiles_hbm.at[g, k], tiles.at[g, k - 1], tile_sem.at[g, k - 1]
        )

    for copy in small:
        copy.start()
    for g in range(blocks):
        jacobi_copy(g).start()
    small[0].wait()

    @pl.loop(0, blocks)
    def _(g):
        @pl.loop(1, counts[g])
        def _(k):
            tile_copy(g, k).start(priority=1)

    @pl.loop(0, blocks)
    def _(g):
        @pl.loop(counts[g], slots)
        def _(k):
            tiles[g, k - 1] = jnp.zeros((width, width), F32)

    small[1].wait()
    base = cols[0, 0]
    me = base // blocks
    spot[0] = me // 2
    spot[1] = me % 2
    spot[2] = (me // 2) % 2
    for g in range(blocks):
        for k in range(slots):
            ahead = cols[g, k] - base
            ahead = jnp.where(ahead < 0, ahead + count * blocks, ahead)
            place[g, k] = jnp.clip(ahead, 0, (BAND + 1) * blocks - 1)
            live[g, k] = (k < counts[g]).astype(jnp.int32)
    spread[...] = jnp.zeros_like(spread)
    small[2].wait()

    every = []
    for g in range(blocks):
        jacobi_copy(g).wait()
        columns = times_row(
            lambda i: jacobi[g, 8 * i : 8 * i + 8, :], right[g : g + 1, :], width
        )
        z[g : g + 1, :] = columns_to_row(columns, width)
        every.append(columns)
    for g in range(blocks):
        columns = every[g]

        @pl.loop(1, counts[g])
        def _(k):
            tile_copy(g, k).wait()

        scatter_products(tiles, place, live, g, columns, slots, width, spread)
    near[...] = spread[:blocks]
    sums = jnp.sum(spread[blocks:], axis=1)
    one, two = sums[:blocks], sums[blocks:]
    _, _, odd = where_am_i(spot)
    rows = z[...]
    one_out[...] = one
    back_out[...] = rows
    odd_out[...] = jnp.where(odd, two, rows)
    even_out[...] = jnp.where(odd, rows, two)


def diagonal_product(blocks, width, diagonal, rows, out):
    for g in range(blocks):
        columns = times_row(
            lambda i: diagonal[g, 8 * i : 8 * i + 8, :], rows[g : g + 1, :], width
        )
        out[g : g + 1, :] = columns_to_row(columns, width)


def first_diagonal_kernel(blocks, width, tiles_hbm, z, near, diagonal, near_out, sem):
    copies = [
        pltpu.make_async_copy(tiles_hbm.at[g, 0], diagonal.at[g], sem.at[g])
        for g in range(blocks)
    ]
    for copy in copies:
        copy.start()
    for copy in copies:
        copy.wait()
    diagonal_product(blocks, width, diagonal, z, near_out)
    near_out[...] = near_out[...] + jnp.sum(near[...], axis=1)


def join_kernel(spot, near, forward_in, odd_in, back_in, even_in, known, one, two):
    _, _, odd = where_am_i(spot)
    one[...] = back_in[...]
    two[...] = jnp.where(odd, odd_in[...], even_in[...])
    known[...] = near[...] + forward_in[...] + jnp.where(odd, even_in[...], odd_in[...])


def spread_rows(wide, rows, first):
    for i in range(rows.shape[0]):
        wide[first + i, :, :] = jnp.broadcast_to(rows[i : i + 1], wide.shape[1:])


def middle_kernel(blocks, slots, width,
                  place, live, tiles, jacobi, z, known, one, two, right,
                  image, swap, far, near, wide, spread):
    lanes = padded(width)
    spread_rows(wide, z[...], 0)
    spread_rows(wide, one[...], blocks)
    spread_rows(wide, two[...], 2 * blocks)
    spread[...] = jnp.zeros_like(spread)
    for g in range(blocks):
        columns = upper_columns(tiles, place, live, wide, g, slots, width)
        image[g : g + 1, :] = known[g : g + 1, :] + columns_to_row(columns, width)
    q = image[...]
    size = jnp.max(jnp.max(jnp.abs(q), axis=1, keepdims=True), axis=0, keepdims=True)
    size = jnp.where(size > TINY, size, 1.0)
    scaled = q * (1.0 / size)
    for g in range(blocks):
        columns = times_row(
            lambda i: jacobi[g, 8 * i : 8 * i + 8, :], scaled[g : g + 1, :], width
        )
        swap[g : g + 1, :] = columns_to_row(columns, width)
        scatter_products(tiles, place, live, g, columns, slots, width, spread)
    sums = jnp.sum(spread[...], axis=1)
    far[...] = sums[2 * blocks :]
    near[...] = sums[:blocks]
    swap[blocks : 2 * blocks, :] = sums[blocks : 2 * blocks]
    values = [size, total(right[...] * z[:, :width]), total(z[...] * q)]
    for i, value in enumerate(values):
        swap[2 * blocks + i : 2 * blocks + i + 1, :] = jnp.broadcast_to(value, (1, lanes))


def second_diagonal_kernel(blocks, width, right, diagonal_tiles, image, swap, near, near_out, out):
    w = swap[:blocks, :]
    diagonal_product(blocks, width, diagonal_tiles, swap, near_out)
    diagonal = near_out[...]
    values = [
        total(right[...] * w[:, :width]),
        total(image[...] * w),
        total(w * (diagonal + 2.0 * near[...])),
    ]
    near_out[...] = diagonal + near[...]
    out[...] = lay_scalars(values, 128, 0)


def fold(head, other, width, extra):
    tail = width - 256
    lane = iota((head.shape[0], 128), 1)
    last = jnp.where(lane < tail, head[:, 256:384], pltpu.roll(other[:, 256:384], tail, 1))
    last = jnp.where(lane < 2 * tail, last, extra)
    return head[:, :128], head[:, 128:256], other[:, :128], other[:, 128:256], last


def unfold_first(part, width):
    tail = width - 256
    last = jnp.where(iota(part.shape[1:], 1) < tail, part[4], 0.0)
    return jnp.concatenate([part[0], part[1], last], axis=1)


def unfold_second(part, width):
    tail = width - 256
    last = jnp.where(iota(part.shape[1:], 1) < tail, pltpu.roll(part[4], 128 - tail, 1), 0.0)
    return jnp.concatenate([part[2], part[3], last], axis=1)


def gather_kernel(blocks, width, spot, swap, swapped, far, dots, out):
    _, second, _ = where_am_i(spot)
    rows, other = swap[...], swapped[...]

    def at(block, i):
        return block[2 * blocks + i : 2 * blocks + i + 1]

    mine, theirs = at(rows, 0), at(other, 0)
    scale = jnp.where(second, mine, jnp.maximum(mine, theirs))
    sent = far[...] * (mine / scale) + jnp.where(
        second, 0.0, other[blocks : 2 * blocks] * (theirs / scale)
    )
    crossing = total(rows[blocks : 2 * blocks] * other[:blocks])
    values = [
        mine[:, :128],
        scale[:, :128],
        (at(rows, 1) + at(other, 1))[:, :128],
        (at(rows, 2) + at(other, 2))[:, :128],
        dots[0:1, 0:1],
        dots[0:1, 1:2] / mine[:, :1],
        at(rows, 2)[:, :128],
        dots[0:1, 2:3],
        jnp.where(second, 0.0, 2.0 * crossing),
        theirs[:, :128],
    ]
    extra = lay_scalars(values, 128, 2 * (width - 256))
    parts = fold(rows[:blocks], sent, width, extra)
    for e in range(out.shape[0]):
        for i, part in enumerate(parts):
            out[e, i] = part


def gather_order(chips):
    low, high = chips // 4, chips - chips // 4
    half = chips // 2
    return [
        *range(high - 1, half - 1, -1),
        *range(chips - 1, high - 1, -1),
        *range(low - 1, -1, -1),
        *range(half - 1, low - 1, -1),
    ]


def gather_place(chip, chips):
    low, high = chips // 4, chips - chips // 4
    half = chips // 2
    upper = jnp.where(chip >= high, high - half + chips - 1 - chip, high - 1 - chip)
    lower = jnp.where(chip >= low, chips - 1 - chip + low, chips - half + low - 1 - chip)
    return jnp.where(chip >= half, upper, lower)


def after_kernel(spot, gathered, out):
    chips = gathered.shape[0]
    chip, _, _ = where_am_i(spot)
    out[...] = gathered[gather_place(jnp.where(chip == chips - 1, 0, chip + 1), chips)]


def sums_kernel(blocks, width, gathered, out):
    chips = gathered.shape[0]
    tail = width - 256
    order = gather_order(chips)
    places = [order.index(c) for c in range(chips)]
    table = jnp.concatenate([gathered[e, 4, 0:1, :] for e in places], axis=0)
    later = jnp.concatenate([table[1:], table[:1]], axis=0)

    def at(i, rows=table):
        return rows[:, 2 * tail + i : 2 * tail + i + 1]

    def chips_total(value):
        return jnp.sum(value, axis=0, keepdims=True)

    norm = chips_total(at(2))
    along = chips_total(at(3))
    alpha = norm / along
    size = alpha * at(0)
    fresh = chips_total(size * (size * at(5) - at(4)) - alpha * at(6))
    diagonal = chips_total(
        size * (size * at(7) + (alpha * at(9)) * at(8) - 2.0 * at(0) * at(5))
    )
    weight = (alpha * at(1)) * (alpha * at(0, later))
    inside = iota((blocks, 128), 1) < tail
    lines = []
    for e in range(chips):
        n = (e + 1) % chips
        here, there = gathered[places[e]], gathered[places[n]]
        ends = jnp.where(inside, pltpu.roll(here[4], 128 - tail, 1) * there[4], 0.0)
        pair = here[2] * there[0] + here[3] * there[1] + ends
        lines.append(jnp.sum(pair, axis=0, keepdims=True))
    edges = total(jnp.concatenate(lines, axis=0) * weight)
    values = [fresh, diagonal + 2.0 * edges, norm, along, alpha, 1.0 / norm, along / norm]
    for i, value in enumerate(values):
        out[i : i + 1, :] = jnp.broadcast_to(value, (1, out.shape[1]))


def prepare_kernel(blocks, width, spot, swap, swapped, near, gathered, next_part, sums,
                   known, scaled, factor, wide):
    chips = gathered.shape[0]
    chip, second, _ = where_am_i(spot)
    tail = width - 256
    before = gathered[gather_place(jnp.where(chip == 0, chips - 1, chip - 1), chips)]
    ahead = next_part[...]
    alpha = sums[4:5, :]

    def at(part, i):
        return alpha * part[4, 0:1, 2 * tail + i : 2 * tail + i + 1]

    mine = alpha * swap[2 * blocks : 2 * blocks + 1, :]
    theirs = alpha * swapped[2 * blocks : 2 * blocks + 1, :]
    w = swap[:blocks, :] * mine
    scaled[...] = w
    factor[...] = at(ahead, 9)
    spread_rows(wide, w, 0)
    spread_rows(wide, swapped[:blocks, :] * theirs, blocks)
    spread_rows(wide, unfold_first(ahead, width) * at(ahead, 0), 2 * blocks)
    here = near[...] * mine + unfold_second(before, width) * at(before, 1)
    known[...] = here + jnp.where(second, swapped[blocks : 2 * blocks, :] * theirs, 0.0)


def later_kernel(blocks, slots, width,
                 place, live, spot, tiles, known, factor, ready, next_other,
                 product, wide):
    _, second, _ = where_am_i(spot)
    wide[...] = ready[...]

    @pl.when(second)
    def _():
        spread_rows(wide, unfold_first(next_other[...], width) * factor[...], blocks)

    for g in range(blocks):
        columns = upper_columns(tiles, place, live, wide, g, slots, width)
        product[g : g + 1, :] = known[g : g + 1, :] + columns_to_row(columns, width)


def end_kernel(blocks, width, right, z_ref, image, product, scaled, sums, sums_other,
               update, residual):
    norm, along = sums[2:3, :], sums[3:4, :]
    alpha = sums[4:5, :]
    fresh = norm + (sums[0:1, :] + sums_other[0:1, :])
    curved = along + (sums[1:2, :] + sums_other[1:2, :])
    ratio = fresh * sums[5:6, :]
    step = fresh / (curved - ratio * (fresh * sums[6:7, :]))
    z, q = z_ref[...], image[...]
    z_next = z - scaled[...]
    update[...] = (alpha * z + step * (z_next + ratio * z))[:, :width]
    r_next = right[...] - (alpha * q)[:, :width]
    residual[...] = r_next - (step * ((q - product[...]) + ratio * q))[:, :width]


def on_device(right_side, schur_tiles, block_cols, tile_counts, jacobi_inverse):
    count = lax.axis_size(AXIS)
    blocks, slots, width, _ = schur_tiles.shape
    lanes = padded(width)
    chips = count // 2
    vmem = pl.BlockSpec(memory_space=pltpu.VMEM)
    smem = pl.BlockSpec(memory_space=pltpu.SMEM)
    hbm = pl.BlockSpec(memory_space=pltpu.HBM)
    rows = pltpu.VMEM((2 * blocks, lanes), F32)
    half = pltpu.VMEM((blocks, lanes), F32)
    small = pltpu.VMEM((8, lanes), F32)
    more = pltpu.VMEM((4 * blocks, lanes), F32)
    spread = pltpu.VMEM(((BAND + 1) * blocks, 8, lanes), F32)
    index = pltpu.SMEM((blocks, slots), jnp.int32)
    late = pltpu.VMEM((blocks, 8, lanes), F32)

    def call(kernel, sizes, in_specs, out_shape, scratch=(), work=0):
        single = not isinstance(out_shape, list)
        shapes = [out_shape] if single else out_shape
        specs = [
            smem if getattr(shape, "memory_space", None) == pltpu.SMEM else vmem
            for shape in shapes
        ]
        return pl.pallas_call(
            functools.partial(kernel, *sizes),
            in_specs=in_specs,
            out_specs=specs[0] if single else specs,
            out_shape=out_shape,
            scratch_shapes=list(scratch),
            compiler_params=pltpu.CompilerParams(vmem_limit_bytes=VMEM_LIMIT),
            cost_estimate=pl.CostEstimate(
                flops=2 * work * width * width, bytes_accessed=4 * work * width * width, transcendentals=0
            ),
        )

    def swap_cores(value):
        return lax.ppermute(value, AXIS, [(i, i ^ 1) for i in range(count)])

    def swap_chips(odd, value):
        pairs = []
        for i in range(count):
            chip, core = divmod(i, 2)
            step = 1 if (chip % 2 == 1) == odd else -1
            pairs.append((i, 2 * ((chip + step) % chips) + core))
        return lax.ppermute(value, AXIS, pairs)

    sizes = (blocks, slots, width)
    off_chip = [
        pltpu.with_memory_space_constraint(value, pltpu.HBM)
        for value in (block_cols, tile_counts, right_side, jacobi_inverse, schur_tiles)
    ]
    jacobi, tiles, right, place, live, spot, z, near, one_out, odd_out, back_out, even_out = call(
        begin_kernel, sizes + (count,), [hbm] * 5,
        [
            pltpu.VMEM(jacobi_inverse.shape, F32),
            pltpu.VMEM((blocks, slots - 1, width, width), F32),
            pltpu.VMEM(right_side.shape, F32),
            index, index, pltpu.SMEM((4,), jnp.int32),
            half, late, half, half, half, half,
        ],
        [
            pltpu.SMEM(block_cols.shape, jnp.int32),
            pltpu.SMEM(tile_counts.shape, jnp.int32),
            spread,
            pltpu.SemaphoreType.DMA((3,)),
            pltpu.SemaphoreType.DMA((blocks,)),
            pltpu.SemaphoreType.DMA((blocks, slots - 1)),
        ],
        work=blocks * slots,
    )(*off_chip)
    forward_in = lax.ppermute(one_out, AXIS, [(i, (i + 1) % count) for i in range(count)])
    odd_in = swap_chips(True, odd_out)
    back_in = lax.ppermute(back_out, AXIS, [((i + 1) % count, i) for i in range(count)])
    even_in = swap_chips(False, even_out)
    diagonal, near1 = call(
        first_diagonal_kernel, (blocks, width), [hbm, vmem, vmem],
        [pltpu.VMEM((blocks, width, width), F32), half],
        [pltpu.SemaphoreType.DMA((blocks,))],
        work=blocks,
    )(off_chip[4], z, near)
    known, one, two = call(join_kernel, (), [smem] + [vmem] * 5, [half, half, half])(
        spot, near1, forward_in, odd_in, back_in, even_in
    )
    image, swap, far, near2 = call(
        middle_kernel, sizes, [smem] * 2 + [vmem] * 7, [half, more, half, half], [spread, spread],
        work=3 * blocks * slots,
    )(place, live, tiles, jacobi, z, known, one, two, right)
    swapped = swap_cores(swap)
    near3, dots = call(
        second_diagonal_kernel, (blocks, width), [vmem] * 5, [half, pltpu.VMEM((1, 128), F32)], work=blocks
    )(right, diagonal, image, swap, near2)
    sent = call(
        gather_kernel, (blocks, width), [smem] + [vmem] * 4, pltpu.VMEM((chips, 5, blocks, 128), F32)
    )(spot, swap, swapped, far, dots)
    groups = [[2 * c + core for c in gather_order(chips)] for core in range(2)]
    gathered = lax.all_to_all(sent, AXIS, 0, 0, axis_index_groups=groups)
    next_part = call(after_kernel, (), [smem, vmem], pltpu.VMEM((5, blocks, 128), F32))(spot, gathered)
    next_other = swap_cores(next_part)
    sums = call(sums_kernel, (blocks, width), [vmem], small, work=chips)(gathered)
    sums_other = swap_cores(sums)
    known2, scaled, factor, ready = call(
        prepare_kernel, (blocks, width), [smem] + [vmem] * 6,
        [half, half, pltpu.VMEM((1, lanes), F32), spread],
    )(spot, swap, swapped, near3, gathered, next_part, sums)
    product = call(
        later_kernel, sizes, [smem] * 3 + [vmem] * 5, half, [spread], work=100 * blocks * slots,
    )(place, live, spot, tiles, known2, factor, ready, next_other)
    out = jax.ShapeDtypeStruct(right_side.shape, F32)
    return call(end_kernel, (blocks, width), [vmem] * 7, [out, out])(
        right, z, image, product, scaled, sums, sums_other
    )


def solution(mesh):
    placed = (
        P(AXIS, None),
        P(AXIS, None, None, None),
        P(AXIS, None),
        P(AXIS),
        P(AXIS, None, None),
    )
    return jax.shard_map(
        on_device,
        mesh=mesh,
        in_specs=placed,
        out_specs=(P(AXIS, None), P(AXIS, None)),
        check_vma=False,
    )
```
